32 devices in a mesh: expert: 16 (over z, y, x), half: 1, dp: 2 (over core).
Axes of the slice: x: 2, y: 2, z: 4, core: 2. Of those that a mesh axis runs over, the one named last changes fastest.
Arguments:
- tokens: bfloat16 [4096, 4096], P(('expert', 'dp'), 'half'), may hold values from -6 to 6
- cotangent: bfloat16 [4096, 4096], P(('expert', 'dp'), 'half'), may hold values from -12 to 12
- expert_ids: int32 [4096, 8], P(('expert', 'dp')), may hold values from 0 to 15, as said below
- slot_ids: int32 [4096, 8], P(('expert', 'dp')), may hold values from 0 to 71, as said below
- gate_weights: float32 [4096, 8], P(('expert', 'dp')), may hold values from 0.03 to 0.4
- latent_down: bfloat16 [4096, 1024], P('half', 'dp'), may hold values from -0.09375 to 0.09375
- latent_up: bfloat16 [1024, 4096], P('dp', 'half'), may hold values from -0.1875 to 0.1875
- expert_gate: bfloat16 [16, 1024, 1536], P('expert', 'dp', 'half'), may hold values from -0.1875 to 0.1875
- expert_linear: bfloat16 [16, 1024, 1536], P('expert', 'dp', 'half'), may hold values from -0.1875 to 0.1875
- expert_out: bfloat16 [16, 1536, 1024], P('expert', 'half', 'dp'), may hold values from -0.15625 to 0.15625
Outputs:
- token_grad: bfloat16 [4096, 4096], P(('expert', 'dp'), 'half')
- gate_grad: bfloat16 [16, 1024, 1536], P('expert', 'dp', 'half')
- linear_grad: bfloat16 [16, 1024, 1536], P('expert', 'dp', 'half')
- out_grad: bfloat16 [16, 1536, 1024], P('expert', 'half', 'dp')
The draws below stay inside these ranges and needn't reach their ends.
Inputs may be any that keep to these rules, and one draw needn't show every extreme that they name: `expert_ids`: each row names 8 different experts. In each aligned block of 128 rows (the rows of one device) no expert is named by more than 72 rows, and one expert is named by exactly 72 rows in every block. `slot_ids`: within one aligned block of 128 rows, the entries that name the same expert have different slots.
All inputs are finite; a program needn't handle non-finite values.
Results may differ from the reference program's by a relative error of at most 0.013.
Values may be sent and summed in bfloat16 or wider, within the bound.
No kernel may reach another device: no remote copies, remote signals or barrier semaphores. Data moves between devices by JAX's collectives and lax.ppermute only.
A program may use at most 128 MiB of HBM per device.

```python
import math
import jax
import jax.numpy as jnp
from jax import lax

D = 4096
LATENT = 1024
HIDDEN_SIZE = 1536
TOP = 8
TOK_DEV = 128
EXPERTS = 16
TOKENS = 4096
CAP = 72


def route_tables(key):
    blocks = TOKENS // TOK_DEV
    assigned = TOK_DEV * TOP
    even_load = assigned // EXPERTS
    remainder = assigned % EXPERTS
    ranking = jax.random.permutation(jax.random.fold_in(key, 101), EXPERTS).astype(jnp.int32)
    places = jnp.arange(EXPERTS, dtype=jnp.int32)
    counts = even_load + (places < remainder).astype(jnp.int32)
    first_loads = counts[0::2]
    second = counts[1::2]
    headroom = jnp.minimum(CAP - first_loads, second)
    pair_count = EXPERTS // 2
    limit = jnp.broadcast_to(headroom + 1, (blocks, pair_count))
    moved_loads = jax.random.randint(jax.random.fold_in(key, 102), (blocks, pair_count), 0, limit).astype(jnp.int32)
    moved_loads = moved_loads.at[:, 0].set(CAP - first_loads[0])
    block_loads = jnp.stack([first_loads[None, :] + moved_loads, second[None, :] - moved_loads], axis=2).reshape(blocks, EXPERTS)
    run_ends = jnp.cumsum(block_loads, axis=1)
    run_starts = run_ends - block_loads
    serial = jnp.arange(assigned, dtype=jnp.int32)
    run_index = jnp.sum((serial[None, :, None] >= run_ends[:, None, :]).astype(jnp.int32), axis=2)
    slot_table = serial[None, :] - jnp.take_along_axis(run_starts, run_index, axis=1)
    chosen = ranking[run_index]
    chosen = chosen.reshape(blocks, TOP, TOK_DEV).transpose(0, 2, 1)
    slot_table = slot_table.reshape(blocks, TOP, TOK_DEV).transpose(0, 2, 1)
    row_keys = jax.random.split(jax.random.fold_in(key, 103), blocks)
    shuffle = jax.vmap(lambda subkey: jax.random.permutation(subkey, TOK_DEV))(row_keys).astype(jnp.int32)
    chosen = jnp.take_along_axis(chosen, shuffle[:, :, None], axis=1)
    slot_table = jnp.take_along_axis(slot_table, shuffle[:, :, None], axis=1)
    rotate = jax.random.randint(jax.random.fold_in(key, 104), (blocks, TOK_DEV, 1), 0, TOP).astype(jnp.int32)
    column = (jnp.arange(TOP, dtype=jnp.int32)[None, None, :] + rotate) % TOP
    chosen = jnp.take_along_axis(chosen, column, axis=2)
    slot_table = jnp.take_along_axis(slot_table, column, axis=2)
    return (chosen.reshape(TOKENS, TOP).astype(jnp.int32), slot_table.reshape(TOKENS, TOP).astype(jnp.int32))


def draw_expert_ids(key, part):
    return route_tables(key)[0]


def draw_slot_ids(key, part):
    return route_tables(key)[1]


def shard_levels(key, shape, shards, least, high):
    loudness = 1.0
    for dim, blocks in shards:
        draws = jax.random.uniform(jax.random.fold_in(jax.random.fold_in(key, 6), dim), (blocks,), jnp.float32, least / len(shards), high / len(shards))
        loudness = loudness * jnp.repeat(jnp.exp(draws), shape[dim] // blocks).reshape((-1,) + (1,) * (len(shape) - 1 - dim))
    return loudness


def noise(key, shape, spread, most, shards=(), kind=jnp.bfloat16):
    loudness = shard_levels(key, shape, shards, -0.22, 0.18) if shards else 1.0
    result = jax.random.normal(key, shape, jnp.float32) * spread * loudness
    return jnp.minimum(jnp.maximum(result, -most), most).astype(kind)


def setup_inputs(seed: int = 0) -> dict:
    keys = jax.random.split(jax.random.key(seed), 11)
    return {
        "tokens": noise(keys[0], (TOKENS, D), 1.0, 6.0, ((0, 32),)),
        "cotangent": noise(keys[1], (TOKENS, D), 2.0, 12.0, ((0, 32),)),
        "expert_ids": draw_expert_ids(jax.random.fold_in(keys[10], 71), 0),
        "slot_ids": draw_slot_ids(jax.random.fold_in(keys[10], 71), 0),
        "gate_weights": jnp.clip(jnp.exp(math.log(0.4) - 2.5902672 * jax.random.uniform(keys[4], (TOKENS, TOP), jnp.float32) ** shard_levels(keys[4], (TOKENS, TOP), ((0, 32),), -0.2, 0.2)), 0.03, 0.4),
        "latent_down": noise(keys[5], (D, LATENT), D ** -0.5, 0.09375, ((1, 2),)),
        "latent_up": noise(keys[6], (LATENT, D), LATENT ** -0.5, 0.1875, ((0, 2),)),
        "expert_gate": noise(keys[7], (EXPERTS, LATENT, HIDDEN_SIZE), LATENT ** -0.5, 0.1875, ((0, 16), (1, 2))),
        "expert_linear": noise(keys[8], (EXPERTS, LATENT, HIDDEN_SIZE), LATENT ** -0.5, 0.1875, ((0, 16), (1, 2))),
        "expert_out": noise(keys[9], (EXPERTS, HIDDEN_SIZE, LATENT), HIDDEN_SIZE ** -0.5, 0.15625, ((0, 16), (2, 2))),
    }


def reference(tokens, cotangent, expert_ids, slot_ids, gate_weights, latent_down, latent_up, expert_gate, expert_linear, expert_out):
    latent = jnp.dot(tokens, latent_down, preferred_element_type=jnp.float32).astype(jnp.bfloat16)
    back_latent = lax.dot_general(cotangent, latent_up, (((1,), (1,)), ((), ())), preferred_element_type=jnp.float32)
    per_expert = (TOKENS // TOK_DEV) * CAP
    assigned = TOKENS * TOP
    token_index = jnp.arange(TOKENS, dtype=jnp.int32)
    block_of = token_index // TOK_DEV
    where_to = (expert_ids * per_expert + block_of[:, None] * CAP + slot_ids).astype(jnp.int32)
    sources = jnp.full((EXPERTS * per_expert,), assigned, jnp.int32)
    sources = sources.at[where_to.reshape(-1)].set(jnp.arange(assigned, dtype=jnp.int32))
    sources = sources.reshape(EXPERTS, per_expert)
    gate_flat = gate_weights.reshape(-1)

    def one_expert(operands):
        source_rows, w_gate, w_linear, w_out = operands
        filled = source_rows < assigned
        clamped = jnp.minimum(source_rows, assigned - 1)
        token_pos = clamped // TOP
        inputs = jnp.where(filled[:, None], latent[token_pos], jnp.zeros((), jnp.bfloat16))
        upstream = jnp.where(filled[:, None], gate_flat[clamped][:, None] * back_latent[token_pos], jnp.zeros((), jnp.float32)).astype(jnp.bfloat16)
        pre_gate = jnp.dot(inputs, w_gate, preferred_element_type=jnp.float32)
        pre_linear = jnp.dot(inputs, w_linear, preferred_element_type=jnp.float32)
        grad_hidden = lax.dot_general(upstream, w_out, (((1,), (1,)), ((), ())), preferred_element_type=jnp.float32)
        logistic = jax.nn.sigmoid(pre_gate)
        hidden = (pre_gate * logistic * pre_linear).astype(jnp.bfloat16)
        gate_delta = (grad_hidden * pre_linear * logistic * (1.0 + pre_gate * (1.0 - logistic))).astype(jnp.bfloat16)
        linear_delta = (grad_hidden * pre_gate * logistic).astype(jnp.bfloat16)
        grad_gate = lax.dot_general(inputs, gate_delta, (((0,), (0,)), ((), ())), preferred_element_type=jnp.float32)
        grad_linear = lax.dot_general(inputs, linear_delta, (((0,), (0,)), ((), ())), preferred_element_type=jnp.float32)
        grad_out = lax.dot_general(hidden, upstream, (((0,), (0,)), ((), ())), preferred_element_type=jnp.float32)
        row_grad = lax.dot_general(gate_delta, w_gate, (((1,), (1,)), ((), ())), preferred_element_type=jnp.float32)
        row_grad = row_grad + lax.dot_general(linear_delta, w_linear, (((1,), (1,)), ((), ())), preferred_element_type=jnp.float32)
        return grad_gate, grad_linear, grad_out, row_grad.astype(jnp.bfloat16)

    gate_grad, linear_grad, out_grad, row_grads = lax.map(one_expert, (sources, expert_gate, expert_linear, expert_out))
    picked = row_grads.reshape(EXPERTS * per_expert, LATENT)[where_to]
    latent_grad = jnp.sum(picked.astype(jnp.float32), axis=1).astype(jnp.bfloat16)
    token_grad = lax.dot_general(latent_grad, latent_down, (((1,), (1,)), ((), ())), preferred_element_type=jnp.float32)
    return token_grad.astype(jnp.bfloat16), gate_grad.astype(jnp.bfloat16), linear_grad.astype(jnp.bfloat16), out_grad.astype(jnp.bfloat16)
```

```python
import functools

import jax
import jax.numpy as jnp
from jax import lax
from jax.experimental import pallas as pl
from jax.experimental.pallas import tpu as pltpu
from jax.sharding import PartitionSpec as P

BF = jnp.bfloat16
F32 = jnp.float32
PLANES = 4
VMEM_LIMIT = 56 * 1024 * 1024
ROWS = (((0,), (0,)), ((), ()))
LAST = (((1,), (1,)), ((), ()))


def pad16(n):
    return (n + 15) // 16 * 16


def params():
    return pltpu.CompilerParams(vmem_limit_bytes=VMEM_LIMIT)


def cost(flops, moved):
    return pl.CostEstimate(flops=int(flops), bytes_accessed=int(moved), transcendentals=0)


def whole(shape):
    return pl.BlockSpec(shape, lambda *_: (0,) * len(shape))


def one_hot(meta_ref, picks, inner, cap, padded, weighted):
    me = lax.axis_index("expert")
    place = lax.rem(me, inner)
    first = me - place
    tokens = meta_ref.shape[1]
    slot = lax.broadcasted_iota(jnp.int32, (padded, tokens), 0)
    targets = []
    for k in range(inner):
        base = (first + lax.bitwise_xor(place, k)) * cap
        targets.append(jnp.where(slot < cap, slot + base, -1))
    target = jnp.concatenate(targets, axis=0).astype(F32)
    mark = jnp.zeros(target.shape, F32)
    weight = jnp.zeros(target.shape, F32)
    for j in range(picks):
        equal = target == meta_ref[j : j + 1, :]
        mark = jnp.where(equal, 1.0, mark)
        if weighted:
            weight = jnp.where(equal, meta_ref[picks + j : picks + j + 1, :], weight)
    return mark, (jnp.sum(weight, axis=1, keepdims=True) if weighted else None)


def select_body(picks, inner, cap, padded, weighted, meta_ref, block_ref, *piece_refs):
    mark, weight = one_hot(meta_ref, picks, inner, cap, padded, weighted)
    rows = jnp.dot(mark.astype(BF), block_ref[...], preferred_element_type=F32)
    if weighted:
        rows = rows * weight
    for k in range(inner):
        piece_refs[k][...] = rows[k * padded : k * padded + cap, :].astype(BF)


def select(meta, block, inner, cap, weighted):
    picks = meta.shape[0] // 2
    padded = pad16(cap)
    tokens, width = block.shape
    return pl.pallas_call(
        functools.partial(select_body, picks, inner, cap, padded, weighted),
        out_shape=[jax.ShapeDtypeStruct((cap, width), BF)] * inner,
        compiler_params=params(),
        cost_estimate=cost(2 * inner * padded * tokens * width, 4 * tokens * width),
        name="select_back" if weighted else "select_latent",
    )(meta, block)


def assemble(piece_refs, out_ref, cap, padded):
    for i, ref in enumerate(piece_refs):
        if padded > cap:
            out_ref[(i + 1) * padded - 16 : (i + 1) * padded, :] = jnp.zeros(
                (16, out_ref.shape[1]), out_ref.dtype
            )
        out_ref[i * padded : i * padded + cap, :] = ref[...]


def expand_body(picks, inner, cap, padded, meta_ref, *refs):
    piece_refs, out_ref, held = refs[:inner], refs[inner], refs[inner + 1]
    assemble(piece_refs, held, cap, padded)
    mark, _ = one_hot(meta_ref, picks, inner, cap, padded, False)
    out_ref[...] = lax.dot_general(
        mark.astype(BF), held[...], ROWS, preferred_element_type=F32
    ).astype(out_ref.dtype)


def expand(meta, pieces, dtype):
    picks, tokens = meta.shape[0] // 2, meta.shape[1]
    inner = len(pieces)
    cap, width = pieces[0].shape
    padded = pad16(cap)
    return pl.pallas_call(
        functools.partial(expand_body, picks, inner, cap, padded),
        out_shape=jax.ShapeDtypeStruct((tokens, width), dtype),
        scratch_shapes=[pltpu.VMEM((inner * padded, width), BF)],
        compiler_params=params(),
        cost_estimate=cost(2 * inner * padded * tokens * width, 4 * tokens * width),
        name="expand_rows",
    )(meta, *pieces)


def forward_body(count, cap, padded, *refs):
    piece_refs = refs[:count]
    gate_m, gate_o, linear_m, linear_o, x_ref, pre_gate_ref, pre_linear_ref = refs[count:]

    @pl.when(pl.program_id(0) == 0)
    def _():
        assemble(piece_refs, x_ref, cap, padded)

    half = x_ref.shape[1] // 2
    mine, other = x_ref[:, :half], x_ref[:, half:]
    for m_ref, o_ref, out in ((gate_m, gate_o, pre_gate_ref), (linear_m, linear_o, pre_linear_ref)):
        out[...] = jnp.dot(mine, m_ref[...], preferred_element_type=F32) + jnp.dot(
            other, o_ref[...], preferred_element_type=F32
        )


def forward(pieces, weights, tile):
    count = len(pieces)
    cap, width = pieces[0].shape
    padded = pad16(cap)
    rows = count * padded
    hidden = weights[0].shape[1]
    column = lambda j: (0, j)
    return pl.pallas_call(
        functools.partial(forward_body, count, cap, padded),
        grid=(hidden // tile,),
        in_specs=[whole((cap, width))] * count + [pl.BlockSpec((width // 2, tile), column)] * 4,
        out_specs=[whole((rows, width))] + [pl.BlockSpec((rows, tile), column)] * 2,
        out_shape=[jax.ShapeDtypeStruct((rows, width), BF)]
        + [jax.ShapeDtypeStruct((rows, hidden), F32)] * 2,
        compiler_params=params(),
        cost_estimate=cost(4 * rows * width * hidden, 8 * rows * hidden + 4 * width * hidden),
        name="forward_rows",
    )(*pieces, *weights)


def backward_body(count, cap, padded, *refs):
    piece_refs = refs[:count]
    (pre_gate_ref, pre_linear_ref, out_m, out_o, gate_m, gate_o, linear_m, linear_o) = refs[
        count : count + 8
    ]
    b_ref, gate_delta_ref, linear_delta_ref, hidden_ref = refs[count + 8 : count + 12]
    row_refs = refs[count + 12 : 2 * count + 12]
    total = refs[2 * count + 12]
    step = pl.program_id(0)

    @pl.when(step == 0)
    def _():
        assemble(piece_refs, b_ref, cap, padded)

    half = b_ref.shape[1] // 2
    grad_hidden = lax.dot_general(
        b_ref[:, :half], out_m[...], LAST, preferred_element_type=F32
    ) + lax.dot_general(b_ref[:, half:], out_o[...], LAST, preferred_element_type=F32)
    pre_gate, pre_linear = pre_gate_ref[...], pre_linear_ref[...]
    logistic = jax.nn.sigmoid(pre_gate)
    scaled = pre_gate * logistic
    hidden_ref[...] = (scaled * pre_linear).astype(BF)
    linear_delta = (grad_hidden * scaled).astype(BF)
    gate_delta = (
        grad_hidden * pre_linear * logistic * (1.0 + pre_gate * (1.0 - logistic))
    ).astype(BF)
    gate_delta_ref[...] = gate_delta
    linear_delta_ref[...] = linear_delta
    parts = []
    for gate, linear in ((gate_m, linear_m), (gate_o, linear_o)):
        parts.append(
            lax.dot_general(gate_delta, gate[...], LAST, preferred_element_type=F32)
            + lax.dot_general(linear_delta, linear[...], LAST, preferred_element_type=F32)
        )

    @pl.when(step == 0)
    def _():
        total[:, :half] = parts[0]
        total[:, half:] = parts[1]

    @pl.when(step > 0)
    def _():
        total[:, :half] += parts[0]
        total[:, half:] += parts[1]

    @pl.when(step == pl.num_programs(0) - 1)
    def _():
        for i, ref in enumerate(row_refs):
            ref[...] = total[i * padded : i * padded + cap, :].astype(BF)


def backward(pieces, pre_gate, pre_linear, out_weights, weights, tile):
    count = len(pieces)
    cap, width = pieces[0].shape
    padded = pad16(cap)
    rows = count * padded
    hidden = pre_gate.shape[1]
    column = lambda j: (0, j)
    tiles = pl.BlockSpec((rows, tile), column)
    results = pl.pallas_call(
        functools.partial(backward_body, count, cap, padded),
        grid=(hidden // tile,),
        in_specs=[whole((cap, width))] * count
        + [tiles] * 2
        + [pl.BlockSpec((tile, width // 2), lambda j: (j, 0))] * 2
        + [pl.BlockSpec((width // 2, tile), column)] * 4,
        out_specs=[whole((rows, width))] + [tiles] * 3 + [whole((cap, width))] * count,
        out_shape=[jax.ShapeDtypeStruct((rows, width), BF)]
        + [jax.ShapeDtypeStruct((rows, hidden), BF)] * 3
        + [jax.ShapeDtypeStruct((cap, width), BF)] * count,
        scratch_shapes=[pltpu.VMEM((rows, width), F32)],
        compiler_params=params(),
        cost_estimate=cost(6 * rows * width * hidden, 14 * rows * hidden + 6 * width * hidden),
        name="backward_rows",
    )(*pieces, pre_gate, pre_linear, *out_weights, *weights)
    return results[:4], results[4:]


def weight_body(groups, add, *refs):
    ins = refs[: 5 * groups]
    at = 5 * groups
    received = refs[at : at + 3] if add else ()
    at += 3 if add else 0
    outs = refs[at : at + 3]
    totals = [None, None, None]
    for g in range(groups):
        x_ref, b_ref, gate_delta_ref, linear_delta_ref, hidden_ref = ins[5 * g : 5 * g + 5]
        for i, (a, b) in enumerate(
            ((x_ref, gate_delta_ref), (x_ref, linear_delta_ref), (hidden_ref, b_ref))
        ):
            term = lax.dot_general(a[...], b[...], ROWS, preferred_element_type=F32)
            totals[i] = term if totals[i] is None else totals[i] + term
    for i in range(3):
        if add:
            totals[i] = totals[i] + received[i][...].astype(F32)
        outs[i][...] = totals[i].astype(BF)


def weight_grads(groups, column, received, tile):
    hidden = groups[0][2].shape[1]
    width = groups[0][0].shape[1]
    in_specs, operands, total_rows = [], [], 0
    for x, b, gate_delta, linear_delta, hid in groups:
        rows = x.shape[0]
        total_rows += rows
        side = pl.BlockSpec((rows, width // 2), lambda j: (0, column))
        tiles = pl.BlockSpec((rows, tile), lambda j: (0, j))
        in_specs += [side, side, tiles, tiles, tiles]
        operands += [x, b, gate_delta, linear_delta, hid]
    wide = pl.BlockSpec((width // 2, tile), lambda j: (0, j))
    tall = pl.BlockSpec((tile, width // 2), lambda j: (j, 0))
    if received:
        in_specs += [wide, wide, tall]
        operands += list(received)
    return pl.pallas_call(
        functools.partial(weight_body, len(groups), bool(received)),
        grid=(hidden // tile,),
        in_specs=in_specs,
        out_specs=[wide, wide, tall],
        out_shape=[jax.ShapeDtypeStruct((width // 2, hidden), BF)] * 2
        + [jax.ShapeDtypeStruct((hidden, width // 2), BF)],
        compiler_params=params(),
        cost_estimate=cost(
            3 * total_rows * width * hidden, 6 * total_rows * hidden + 3 * width * hidden
        ),
        name="weight_grads",
    )(*operands)


def on_device(
    tokens,
    cotangent,
    expert_ids,
    slot_ids,
    gate_weights,
    latent_down,
    latent_up,
    expert_gate,
    expert_linear,
    expert_out,
):
    row_count = tokens.shape[0]
    pick_count = expert_ids.shape[1]
    group_count = lax.axis_size("expert")
    halves = lax.axis_size("half")
    expert_count = group_count * expert_gate.shape[0]
    capacity = min(
        row_count, 2 * ((9 * row_count * pick_count + 16 * expert_count - 1) // (16 * expert_count))
    )
    inner = group_count // PLANES
    tile = 256

    def swap(a):
        return lax.ppermute(a, "dp", [(0, 1), (1, 0)])

    def along(a, shift):
        return lax.ppermute(
            a,
            "expert",
            [
                (z * inner + p, (z + shift) % PLANES * inner + p)
                for z in range(PLANES)
                for p in range(inner)
            ],
        )

    def across(a, k):
        return lax.ppermute(a, "expert", [(i, i ^ k) for i in range(group_count)])

    def join(a):
        return lax.psum(a, "half") if halves > 1 else a

    position = (expert_ids * capacity + slot_ids).astype(F32)
    meta = jnp.concatenate([position, gate_weights], axis=1).T
    metas = [meta] + [along(meta, c) for c in range(1, PLANES)]

    def project(mine, weight, dims):
        def dot(a):
            return join(lax.dot_general(a, weight, dims, preferred_element_type=F32)).astype(BF)

        own = dot(mine)
        return jnp.concatenate([own, swap(dot(swap(mine)))], axis=1)

    latent = project(tokens, latent_down, (((1,), (0,)), ((), ())))
    back = project(cotangent, latent_up, LAST)

    gate, linear, out = expert_gate[0], expert_linear[0], expert_out[0]
    gate_pair, linear_pair, out_pair = (gate, swap(gate)), (linear, swap(linear)), (out, swap(out))
    down_pair = (latent_down, swap(latent_down))

    def spread(block, order, weighted):
        blocks = {0: block}
        for c in order:
            if c:
                blocks[c] = along(block, c)
        pieces = {}
        for c in order:
            parts = select(metas[c], blocks[c], inner, capacity, weighted)
            pieces[c] = [parts[0]] + [across(parts[k], k) for k in range(1, inner)]
        return pieces

    latent_pieces = spread(latent, (0, 1, 3, 2), False)
    back_pieces = spread(back, (2, 3, 0, 1), True)
    groups, partial = [], {}
    for chunks in ((2, 3), (0, 1)):
        x, pre_gate, pre_linear = forward(
            [a for c in chunks for a in latent_pieces[c]], (*gate_pair, *linear_pair), tile
        )
        (b, gate_delta, linear_delta, hid), rows = backward(
            [a for c in chunks for a in back_pieces[c]],
            pre_gate,
            pre_linear,
            out_pair,
            (*gate_pair, *linear_pair),
            tile,
        )
        groups.append((x, b, gate_delta, linear_delta, hid))
        for i, c in enumerate(chunks):
            mine = rows[i * inner : (i + 1) * inner]
            home = [mine[0]] + [across(mine[k], k) for k in range(1, inner)]
            part = expand(metas[c], home, BF if c else F32)
            partial[c] = along(part, -c) if c else part
    theirs = weight_grads(groups, 1, (), tile)
    grads = weight_grads(groups, 0, [swap(a) for a in theirs], tile)

    total = partial[0]
    for c in range(1, PLANES):
        total = total + partial[c].astype(F32)
    latent_grad = join(total).astype(BF)
    side = latent_grad.shape[1] // 2
    token_grad = lax.dot_general(
        latent_grad[:, :side], down_pair[0], LAST, preferred_element_type=F32
    ) + lax.dot_general(latent_grad[:, side:], down_pair[1], LAST, preferred_element_type=F32)
    return (token_grad.astype(BF), grads[0][None], grads[1][None], grads[2][None])


def solution(mesh):
    in_specs = (
        P(("expert", "dp"), "half"),
        P(("expert", "dp"), "half"),
        P(("expert", "dp"), None),
        P(("expert", "dp"), None),
        P(("expert", "dp"), None),
        P("half", "dp"),
        P("dp", "half"),
        P("expert", "dp", "half"),
        P("expert", "dp", "half"),
        P("expert", "half", "dp"),
    )
    out_specs = (
        P(("expert", "dp"), "half"),
        P("expert", "dp", "half"),
        P("expert", "dp", "half"),
        P("expert", "half", "dp"),
    )
    return jax.shard_map(
        on_device, mesh=mesh, in_specs=in_specs, out_specs=out_specs, check_vma=False
    )
```

```python
import functools

import jax
import jax.numpy as jnp
from jax import lax
from jax.experimental import pallas as pl
from jax.experimental.pallas import tpu as pltpu
from jax.sharding import PartitionSpec as P

BF = jnp.bfloat16
F32 = jnp.float32
PLANES = 4
META = 8
MIB = 1024 * 1024
ROWS = (((0,), (0,)), ((), ()))
LAST = (((1,), (1,)), ((), ()))
ANY = pl.BlockSpec(memory_space=pl.ANY)
VMEM = pl.BlockSpec(memory_space=pltpu.VMEM)


def pad16(n):
    return (n + 15) // 16 * 16


def params(mib):
    return pltpu.CompilerParams(vmem_limit_bytes=mib * MIB)


def cost(flops, moved):
    return pl.CostEstimate(flops=int(flops), bytes_accessed=int(moved), transcendentals=0)


def whole(shape):
    return pl.BlockSpec(shape, lambda *_: (0,) * len(shape))


def join_body(routes, own_ref, other_ref, *refs):
    out_ref = refs[-1]
    tokens, half = own_ref.shape
    out_ref[:tokens, :half] = own_ref[...]
    out_ref[:tokens, half:] = other_ref[...]
    if routes:
        ids_ref, slots_ref, gates_ref = refs[:3]
        gates = gates_ref[...]
        high = gates.astype(BF)
        rest = gates - high.astype(F32)
        middle = rest.astype(BF)
        low = (rest - middle.astype(F32)).astype(BF)
        kinds = [ids_ref[...].astype(F32).astype(BF), slots_ref[...].astype(F32).astype(BF)]
        kinds += [high, middle, low]
        kinds += [jnp.zeros_like(low)] * (META - len(kinds))
        picks = gates.shape[0]
        table = jnp.concatenate([a.astype(F32) for a in kinds], axis=1)
        table = jnp.concatenate(
            [table, jnp.zeros((pad16(picks) - picks, table.shape[1]), F32)], axis=0
        )
        out_ref[tokens:, :] = table.astype(BF)


def join_rows(own, other, routes):
    tokens, half = own.shape
    extra = pad16(routes[0].shape[0]) if routes else 0
    return pl.pallas_call(
        functools.partial(join_body, bool(routes)),
        out_shape=jax.ShapeDtypeStruct((tokens + extra, 2 * half), BF),
        compiler_params=params(8),
        cost_estimate=cost(0, 8 * tokens * half),
        name="join_rows",
    )(own, other, *routes)


def tie_body(block_ref, *refs):
    refs[-1][...] = block_ref[...]


def tie(block, deps):
    return pl.pallas_call(
        tie_body,
        out_shape=jax.ShapeDtypeStruct(block.shape, block.dtype),
        in_specs=[VMEM] + [ANY] * len(deps),
        out_specs=VMEM,
        compiler_params=params(8),
        cost_estimate=cost(0, 4 * block.size),
        name="tie_rows",
    )(block, *deps)


def one_hots(meta_refs, picks, inner, cap, weighted):
    me = lax.axis_index("expert")
    place = lax.rem(me, inner)
    first = me - place
    padded = pad16(len(meta_refs) * cap)
    marks, total = [], None
    for j, ref in enumerate(meta_refs):
        tokens = ref.shape[1] // META
        start = ref.shape[0] - pad16(picks)
        kinds = [
            ref[start:, i * tokens : (i + 1) * tokens].astype(F32)
            for i in range(5 if weighted else 2)
        ]
        held = kinds[0] * cap + kinds[1]
        row = lax.broadcasted_iota(jnp.int32, (padded, tokens), 0)
        inside = jnp.logical_and(row >= j * cap, row < (j + 1) * cap)
        targets = []
        for k in range(inner):
            base = (first + lax.bitwise_xor(place, k)) * cap - j * cap
            targets.append(jnp.where(inside, row + base, -1))
        target = jnp.concatenate(targets, axis=0).astype(F32)
        mark = jnp.zeros(target.shape, F32)
        weight = jnp.zeros(target.shape, F32)
        if weighted:
            gate = kinds[2] + kinds[3] + kinds[4]
        for i in range(picks):
            equal = target == held[i : i + 1, :]
            mark = jnp.where(equal, 1.0, mark)
            if weighted:
                weight = jnp.where(equal, gate[i : i + 1, :], weight)
        marks.append(mark.astype(BF))
        if weighted:
            weight = jnp.sum(weight, axis=1, keepdims=True)
            total = weight if total is None else total + weight
    return marks, total


def select_body(count, picks, inner, cap, weighted, deps, *refs):
    meta_refs, block_refs, piece_refs = refs[:count], refs[count : 2 * count], refs[2 * count + deps :]
    marks, weight = one_hots(meta_refs, picks, inner, cap, weighted)
    tokens = marks[0].shape[1]
    rows = None
    for mark, block_ref in zip(marks, block_refs):
        term = jnp.dot(mark, block_ref[:tokens, :], preferred_element_type=F32)
        rows = term if rows is None else rows + term
    if weighted:
        rows = rows * weight
    padded = pad16(count * cap)
    for k in range(inner):
        piece_refs[k][...] = rows[k * padded : k * padded + count * cap, :].astype(BF)


def select(metas, blocks, picks, inner, cap, weighted, deps):
    count = len(blocks)
    width = blocks[0].shape[1]
    tokens = width // META
    return pl.pallas_call(
        functools.partial(select_body, count, picks, inner, cap, weighted, len(deps)),
        out_shape=[jax.ShapeDtypeStruct((count * cap, width), BF)] * inner,
        in_specs=[VMEM] * (2 * count) + [ANY] * len(deps),
        out_specs=[VMEM] * inner,
        compiler_params=params(10),
        cost_estimate=cost(
            2 * inner * count * count * cap * tokens * width, 8 * count * tokens * width
        ),
        name="select_back" if weighted else "select_latent",
    )(*metas, *blocks, *deps)


def assemble(piece_refs, out_ref):
    rows = piece_refs[0].shape[0]
    padded = pad16(rows)
    for i, ref in enumerate(piece_refs):
        if padded > rows:
            out_ref[(i + 1) * padded - 16 : (i + 1) * padded, :] = jnp.zeros(
                (16, out_ref.shape[1]), out_ref.dtype
            )
        out_ref[i * padded : i * padded + rows, :] = ref[...]


def expand_body(count, picks, inner, cap, deps, *refs):
    meta_refs, piece_refs = refs[:count], refs[count : count + inner]
    out_refs, held = refs[count + inner + deps : -1], refs[-1]
    assemble(piece_refs, held)
    marks, _ = one_hots(meta_refs, picks, inner, cap, False)
    for mark, out_ref in zip(marks, out_refs):
        out_ref[...] = lax.dot_general(
            mark, held[...], ROWS, preferred_element_type=F32
        ).astype(out_ref.dtype)


def expand(metas, pieces, picks, cap, dtypes, deps):
    count, inner = len(metas), len(pieces)
    width = pieces[0].shape[1]
    tokens = width // META
    padded = pad16(count * cap)
    return pl.pallas_call(
        functools.partial(expand_body, count, picks, inner, cap, len(deps)),
        out_shape=[jax.ShapeDtypeStruct((tokens, width), d) for d in dtypes],
        in_specs=[VMEM] * (count + inner) + [ANY] * len(deps),
        out_specs=[VMEM] * count,
        scratch_shapes=[pltpu.VMEM((inner * padded, width), BF)],
        compiler_params=params(10),
        cost_estimate=cost(
            2 * inner * count * padded * tokens * width, 8 * count * tokens * width
        ),
        name="expand_rows",
    )(*metas, *pieces, *deps)


def tile_of(hidden):
    return 512 if hidden % 512 == 0 else 256


def forward_body(count, *refs):
    piece_refs = refs[:count]
    gate_m, gate_o, linear_m, linear_o = refs[count : count + 4]
    x_ref, gate_factor_ref, linear_factor_ref, hidden_ref = refs[count + 4 :]
    assemble(piece_refs, x_ref)
    half, hidden = gate_m.shape
    tile = tile_of(hidden)
    for start in range(0, hidden, tile):
        at = slice(start, start + tile)
        pre_gate = jnp.dot(x_ref[:, :half], gate_m[:, at], preferred_element_type=F32)
        pre_gate += jnp.dot(x_ref[:, half:], gate_o[:, at], preferred_element_type=F32)
        pre_linear = jnp.dot(x_ref[:, :half], linear_m[:, at], preferred_element_type=F32)
        pre_linear += jnp.dot(x_ref[:, half:], linear_o[:, at], preferred_element_type=F32)
        logistic = jax.nn.sigmoid(pre_gate)
        scaled = pre_gate * logistic
        hidden_ref[:, at] = (scaled * pre_linear).astype(BF)
        linear_factor_ref[:, at] = scaled.astype(BF)
        gate_factor_ref[:, at] = (
            pre_linear * logistic * (1.0 + pre_gate * (1.0 - logistic))
        ).astype(BF)


def forward(pieces, gate, linear):
    count = len(pieces)
    size, width = pieces[0].shape
    rows = count * pad16(size)
    hidden = gate[0].shape[1]
    return pl.pallas_call(
        functools.partial(forward_body, count),
        in_specs=[VMEM] * (count + 4),
        out_specs=[VMEM] * 4,
        out_shape=[jax.ShapeDtypeStruct((rows, width), BF)]
        + [jax.ShapeDtypeStruct((rows, hidden), BF)] * 3,
        compiler_params=params(10),
        cost_estimate=cost(4 * rows * width * hidden, 6 * rows * hidden + 4 * width * hidden),
        name="forward_rows",
    )(*pieces, *gate, *linear)


def backward_body(count, deps, *refs):
    piece_refs = refs[:count]
    gate_factor, linear_factor, out_m, out_o = refs[count : count + 4]
    gate_m, gate_o, linear_m, linear_o = refs[count + 4 : count + 8]
    refs = refs[count + 8 + deps :]
    b_ref, gate_delta_ref, linear_delta_ref = refs[:3]
    row_refs, total = refs[3:-1], refs[-1]
    assemble(piece_refs, b_ref)
    hidden, half = out_m.shape
    tile = tile_of(hidden)
    for start in range(0, hidden, tile):
        at = slice(start, start + tile)
        grad = lax.dot_general(b_ref[:, :half], out_m[at, :], LAST, preferred_element_type=F32)
        grad += lax.dot_general(b_ref[:, half:], out_o[at, :], LAST, preferred_element_type=F32)
        gate_delta_ref[:, at] = (grad * gate_factor[:, at].astype(F32)).astype(BF)
        linear_delta_ref[:, at] = (grad * linear_factor[:, at].astype(F32)).astype(BF)
    for start, gate, linear in ((0, gate_m, linear_m), (half, gate_o, linear_o)):
        part = lax.dot_general(gate_delta_ref[...], gate[...], LAST, preferred_element_type=F32)
        part += lax.dot_general(
            linear_delta_ref[...], linear[...], LAST, preferred_element_type=F32
        )
        total[:, start : start + half] = part
    size = row_refs[0].shape[0]
    for i, ref in enumerate(row_refs):
        start = i * pad16(size)
        ref[...] = total[start : start + size, :].astype(BF)


def backward(pieces, gate_factor, linear_factor, out, gate, linear, deps):
    count = len(pieces)
    size, width = pieces[0].shape
    rows = count * pad16(size)
    hidden = gate_factor.shape[1]
    results = pl.pallas_call(
        functools.partial(backward_body, count, len(deps)),
        in_specs=[VMEM] * (count + 8) + [ANY] * len(deps),
        out_specs=[VMEM] * (3 + count),
        out_shape=[jax.ShapeDtypeStruct((rows, width), BF)]
        + [jax.ShapeDtypeStruct((rows, hidden), BF)] * 2
        + [jax.ShapeDtypeStruct((size, width), BF)] * count,
        scratch_shapes=[pltpu.VMEM((rows, width), F32)],
        compiler_params=params(10),
        cost_estimate=cost(6 * rows * width * hidden, 8 * rows * hidden + 6 * width * hidden),
        name="backward_rows",
    )(*pieces, gate_factor, linear_factor, *out, *gate, *linear, *deps)
    return results[:3], results[3:]


def weight_body(groups, column, add, deps, *refs):
    ins = refs[: 5 * groups]
    at = 5 * groups
    received = refs[at : at + 2]
    outs = refs[at + deps + (2 if add else 0) :]
    width, hidden = ins[0].shape[1], ins[2].shape[1]
    half, tile = width // 2, tile_of(hidden)
    side = slice(column * half, (column + 1) * half)
    for start in range(0, hidden, tile):
        at = slice(start, start + tile)
        totals = [None, None, None]
        for g in range(groups):
            x_ref, b_ref, gate_delta, linear_delta, hid = ins[5 * g : 5 * g + 5]
            for i, (a, b) in enumerate(
                (
                    (x_ref[:, side], gate_delta[:, at]),
                    (x_ref[:, side], linear_delta[:, at]),
                    (hid[:, at], b_ref[:, side]),
                )
            ):
                term = lax.dot_general(a, b, ROWS, preferred_element_type=F32)
                totals[i] = term if totals[i] is None else totals[i] + term
        if add:
            totals[0] += received[0][:half, at].astype(F32)
            totals[1] += received[0][half:, at].astype(F32)
            totals[2] += received[1][at, :].astype(F32)
            outs[0][:, at] = totals[0].astype(BF)
            outs[1][:, at] = totals[1].astype(BF)
            outs[2][at, :] = totals[2].astype(BF)
        else:
            outs[0][:half, at] = totals[0].astype(BF)
            outs[0][half:, at] = totals[1].astype(BF)
            outs[1][at, :] = totals[2].astype(BF)


def weight_grads(groups, column, received, deps):
    hidden = groups[0][2].shape[1]
    width = groups[0][0].shape[1]
    half = width // 2
    operands = [a for group in groups for a in group] + list(received)
    total_rows = sum(group[0].shape[0] for group in groups)
    sizes = [(half, hidden), (half, hidden)] if received else [(width, hidden)]
    sizes.append((hidden, half))
    return pl.pallas_call(
        functools.partial(weight_body, len(groups), column, bool(received), len(deps)),
        in_specs=[VMEM] * len(operands) + [ANY] * len(deps),
        out_specs=[VMEM] * len(sizes),
        out_shape=[jax.ShapeDtypeStruct(s, BF) for s in sizes],
        compiler_params=params(10),
        cost_estimate=cost(
            3 * total_rows * width * hidden, 6 * total_rows * hidden + 3 * width * hidden
        ),
        name="weight_grads",
    )(*operands, *deps)


def on_device(
    tokens,
    cotangent,
    expert_ids,
    slot_ids,
    gate_weights,
    latent_down,
    latent_up,
    expert_gate,
    expert_linear,
    expert_out,
):
    row_count = tokens.shape[0]
    pick_count = expert_ids.shape[1]
    group_count = lax.axis_size("expert")
    halves = lax.axis_size("half")
    expert_count = group_count * expert_gate.shape[0]
    capacity = min(
        row_count, 2 * ((9 * row_count * pick_count + 16 * expert_count - 1) // (16 * expert_count))
    )
    inner = group_count // PLANES

    def swap(a):
        return lax.ppermute(a, "dp", [(0, 1), (1, 0)])

    def along(a, shift):
        return lax.ppermute(
            a,
            "expert",
            [
                (z * inner + p, (z + shift) % PLANES * inner + p)
                for z in range(PLANES)
                for p in range(inner)
            ],
        )

    def across(parts):
        return [parts[0]] + [
            lax.ppermute(parts[k], "expert", [(i, i ^ k) for i in range(group_count)])
            for k in range(1, inner)
        ]

    def summed(a):
        return lax.psum(a, "half") if halves > 1 else a

    def project(mine, weight, dims):
        def dot(a):
            return summed(lax.dot_general(a, weight, dims, preferred_element_type=F32)).astype(BF)

        own = dot(mine)
        return own, swap(dot(swap(mine)))

    gate, linear, out, down = [
        (a, swap(a)) for a in (expert_gate[0], expert_linear[0], expert_out[0], latent_down)
    ]
    latent = join_rows(
        *project(tokens, latent_down, (((1,), (0,)), ((), ()))),
        (expert_ids.T, slot_ids.T, gate_weights.T),
    )
    back = join_rows(*project(cotangent, latent_up, LAST), ())

    def pick(kind, chunks, blocks, deps):
        parts = select(
            [latents[c] for c in chunks],
            [blocks[c] for c in chunks],
            pick_count,
            inner,
            capacity,
            kind == "b",
            deps,
        )
        with jax.named_scope(f"piece_{kind}{chunks[0]}"):
            return across(parts)

    near, far = (0, 1), (2, 3)
    latents = {0: latent}
    for c in (1, 3, 2):
        with jax.named_scope(f"plane_l{c}"):
            latents[c] = along(latent, c)
    near_latent = pick("l", near, latents, [a[1] for a in (gate, linear, out, down)])
    far_latent = pick("l", far, latents, near_latent[1:])
    tied = tie(back, [far_latent[0]])
    backs = {0: back}
    for c in (2, 3):
        with jax.named_scope(f"plane_b{c}"):
            backs[c] = along(tied, c)
    with jax.named_scope("plane_b1"):
        backs[1] = along(tie(tied, [backs[2]]), 1)
    near_x, *near_factors, near_hidden = forward(near_latent, gate, linear)
    far_back = pick("b", far, backs, [near_hidden] + far_latent[1:])
    far_x, *far_factors, far_hidden = forward(far_latent, gate, linear)
    near_back = pick("b", near, backs, [far_hidden])

    far_saved, far_rows = backward(far_back, *far_factors, out, gate, linear, [])
    with jax.named_scope("piece_r2"):
        far_rows = across(far_rows)
    near_saved, near_rows = backward(near_back, *near_factors, out, gate, linear, [far_saved[0]])
    with jax.named_scope("piece_r0"):
        near_rows = across(near_rows)
    groups = [(far_x, *far_saved, far_hidden), (near_x, *near_saved, near_hidden)]

    partial = {}
    partial[2], partial[3] = expand(
        [latents[c] for c in far], far_rows, pick_count, capacity, [BF, BF], []
    )
    theirs = weight_grads(groups, 1, (), [partial[2]])
    partial[0], partial[1] = expand(
        [latents[c] for c in near], near_rows, pick_count, capacity, [F32, BF], [theirs[0]]
    )
    for c in (2, 3, 1):
        with jax.named_scope(f"plane_r{c}"):
            partial[c] = along(partial[c], -c)
    grads = weight_grads(groups, 0, [swap(a) for a in theirs], [partial[0]])

    total = partial[0]
    for c in range(1, PLANES):
        total = total + partial[c].astype(F32)
    latent_grad = summed(total).astype(BF)
    half = latent_grad.shape[1] // 2
    token_grad = lax.dot_general(
        latent_grad[:, :half], down[0], LAST, preferred_element_type=F32
    ) + lax.dot_general(latent_grad[:, half:], down[1], LAST, preferred_element_type=F32)
    return (token_grad.astype(BF), grads[0][None], grads[1][None], grads[2][None])


def solution(mesh):
    in_specs = (
        P(("expert", "dp"), "half"),
        P(("expert", "dp"), "half"),
        P(("expert", "dp"), None),
        P(("expert", "dp"), None),
        P(("expert", "dp"), None),
        P("half", "dp"),
        P("dp", "half"),
        P("expert", "dp", "half"),
        P("expert", "dp", "half"),
        P("expert", "half", "dp"),
    )
    out_specs = (
        P(("expert", "dp"), "half"),
        P("expert", "dp", "half"),
        P("expert", "dp", "half"),
        P("expert", "half", "dp"),
    )
    return jax.shard_map(
        on_device, mesh=mesh, in_specs=in_specs, out_specs=out_specs, check_vma=False
    )
```

```python
import functools

import jax
import jax.numpy as jnp
from jax import lax
from jax.experimental import pallas as pl
from jax.experimental.pallas import tpu as pltpu
from jax.sharding import PartitionSpec as P

BF = jnp.bfloat16
F32 = jnp.float32
PLANES = 4
SIDE = 2
META = 8
SIDE_TIE = True
SCALE = 1
MIB = 1024 * 1024
ROWS = (((0,), (0,)), ((), ()))
LAST = (((1,), (1,)), ((), ()))
ANY = pl.BlockSpec(memory_space=pl.ANY)
VMEM = pl.BlockSpec(memory_space=pltpu.VMEM)


def pad16(n):
    return (n + 15) // 16 * 16


def params(mib):
    return pltpu.CompilerParams(vmem_limit_bytes=mib * MIB)


def cost(flops, moved):
    return pl.CostEstimate(flops=int(flops * SCALE) + 1, bytes_accessed=int(moved * SCALE) + 1, transcendentals=0)


def whole(shape):
    return pl.BlockSpec(shape, lambda *_: (0,) * len(shape))


def join_body(routes, own_ref, other_ref, *refs):
    out_ref = refs[-1]
    tokens, half = own_ref.shape
    out_ref[:tokens, :half] = own_ref[...]
    out_ref[:tokens, half:] = other_ref[...]
    if routes:
        ids_ref, slots_ref, gates_ref = refs[:3]
        gates = gates_ref[...]
        high = gates.astype(BF)
        rest = gates - high.astype(F32)
        middle = rest.astype(BF)
        low = (rest - middle.astype(F32)).astype(BF)
        kinds = [ids_ref[...].astype(F32).astype(BF), slots_ref[...].astype(F32).astype(BF)]
        kinds += [high, middle, low]
        kinds += [jnp.zeros_like(low)] * (META - len(kinds))
        picks = gates.shape[0]
        table = jnp.concatenate([a.astype(F32) for a in kinds], axis=1)
        table = jnp.concatenate(
            [table, jnp.zeros((pad16(picks) - picks, table.shape[1]), F32)], axis=0
        )
        out_ref[tokens:, :] = table.astype(BF)


def join_rows(own, other, routes, deps):
    tokens, half = own.shape
    extra = pad16(routes[0].shape[0]) if routes else 0
    return pl.pallas_call(
        functools.partial(join_body, bool(routes)),
        out_shape=jax.ShapeDtypeStruct((tokens + extra, 2 * half), BF),
        in_specs=[VMEM] * (2 + len(routes)) + [ANY] * len(deps),
        out_specs=VMEM,
        compiler_params=params(8),
        cost_estimate=cost(0, 8 * tokens * half),
        name="join_rows",
    )(own, other, *routes, *deps)


def tie_body(block_ref, *refs):
    refs[-1][...] = block_ref[...]


def tie(block, deps):
    return pl.pallas_call(
        tie_body,
        out_shape=jax.ShapeDtypeStruct(block.shape, block.dtype),
        in_specs=[VMEM] + [ANY] * len(deps),
        out_specs=VMEM,
        compiler_params=params(8),
        cost_estimate=cost(0, 4 * block.size),
        name="tie_rows",
    )(block, *deps)


def one_hots(meta_refs, picks, fan, cap, weighted):
    me = lax.axis_index("expert")
    padded = pad16(len(meta_refs) * cap)
    marks, total = [], None
    for j, ref in enumerate(meta_refs):
        tokens = ref.shape[1] // META
        start = ref.shape[0] - pad16(picks)
        kinds = [
            ref[start:, i * tokens : (i + 1) * tokens].astype(F32)
            for i in range(5 if weighted else 2)
        ]
        held = kinds[0] * cap + kinds[1]
        row = lax.broadcasted_iota(jnp.int32, (padded, tokens), 0)
        inside = jnp.logical_and(row >= j * cap, row < (j + 1) * cap)
        targets = []
        for k in range(fan):
            base = lax.bitwise_xor(me, SIDE * k) * cap - j * cap
            targets.append(jnp.where(inside, row + base, -1))
        target = jnp.concatenate(targets, axis=0).astype(F32)
        mark = jnp.zeros(target.shape, F32)
        weight = jnp.zeros(target.shape, F32)
        if weighted:
            gate = kinds[2] + kinds[3] + kinds[4]
        for i in range(picks):
            equal = target == held[i : i + 1, :]
            mark = jnp.where(equal, 1.0, mark)
            if weighted:
                weight = jnp.where(equal, gate[i : i + 1, :], weight)
        marks.append(mark.astype(BF))
        if weighted:
            weight = jnp.sum(weight, axis=1, keepdims=True)
            total = weight if total is None else total + weight
    return marks, total


def select_body(count, picks, fan, cap, weighted, deps, *refs):
    meta_refs, block_refs, piece_refs = refs[:count], refs[count : 2 * count], refs[2 * count + deps :]
    marks, weight = one_hots(meta_refs, picks, fan, cap, weighted)
    tokens = marks[0].shape[1]
    rows = None
    for mark, block_ref in zip(marks, block_refs):
        term = jnp.dot(mark, block_ref[:tokens, :], preferred_element_type=F32)
        rows = term if rows is None else rows + term
    if weighted:
        rows = rows * weight
    padded = pad16(count * cap)
    for k in range(fan):
        piece_refs[k][...] = rows[k * padded : k * padded + count * cap, :].astype(BF)


def select(metas, blocks, picks, fan, cap, weighted, deps):
    count = len(blocks)
    width = blocks[0].shape[1]
    tokens = width // META
    return pl.pallas_call(
        functools.partial(select_body, count, picks, fan, cap, weighted, len(deps)),
        out_shape=[jax.ShapeDtypeStruct((count * cap, width), BF)] * fan,
        in_specs=[VMEM] * (2 * count) + [ANY] * len(deps),
        out_specs=[VMEM] * fan,
        compiler_params=params(10),
        cost_estimate=cost(
            2 * fan * count * count * cap * tokens * width, 8 * count * tokens * width
        ),
        name="select_back" if weighted else "select_latent",
    )(*metas, *blocks, *deps)


def assemble(piece_refs, out_ref):
    rows = piece_refs[0].shape[0]
    padded = pad16(rows)
    for i, ref in enumerate(piece_refs):
        if padded > rows:
            out_ref[(i + 1) * padded - 16 : (i + 1) * padded, :] = jnp.zeros(
                (16, out_ref.shape[1]), out_ref.dtype
            )
        out_ref[i * padded : i * padded + rows, :] = ref[...]


def bundle_body(parts, held_over, deps, *refs):
    at = sum(len(part[1]) for part in parts)
    ins, refs = refs[:at], refs[at + held_over + deps :]
    outs_count = sum(len(part[2]) for part in parts)
    outs, scratch = refs[:outs_count], refs[outs_count + held_over :]
    for body, operands, results, held in parts:
        body(*ins[: len(operands)], *outs[: len(results)], *scratch[: len(held)])
        ins, outs, scratch = ins[len(operands) :], outs[len(results) :], scratch[len(held) :]


def bundle(parts, through, deps):
    operands = [a for part in parts for a in part[1]]
    shapes = [a for part in parts for a in part[2]]
    sizes = sum(a.size for a in operands)
    results = pl.pallas_call(
        functools.partial(bundle_body, parts, len(through), len(deps)),
        out_shape=shapes + [jax.ShapeDtypeStruct(a.shape, a.dtype) for a in through],
        in_specs=[VMEM] * len(operands) + [ANY] * (len(through) + len(deps)),
        out_specs=[VMEM] * len(shapes) + [ANY] * len(through),
        input_output_aliases={len(operands) + i: len(shapes) + i for i in range(len(through))},
        scratch_shapes=[a for part in parts for a in part[3]],
        compiler_params=params(10),
        cost_estimate=cost(0, 4 * sizes),
        name="return_rows",
    )(*operands, *through, *deps)
    split = []
    for part in parts:
        split.append(results[: len(part[2])])
        results = results[len(part[2]) :]
    return split, results


def copy_body(count, *refs):
    for i in range(count):
        refs[count + i][...] = refs[i][...]


def copies(arrays):
    shapes = [jax.ShapeDtypeStruct(a.shape, a.dtype) for a in arrays]
    return functools.partial(copy_body, len(arrays)), list(arrays), shapes, []


def add_body(count, *refs):
    total = refs[0][...].astype(F32)
    for ref in refs[1:count]:
        total = total + ref[...].astype(F32)
    refs[count][...] = total.astype(refs[count].dtype)


def added(arrays, dtype):
    shape = jax.ShapeDtypeStruct(arrays[0].shape, dtype)
    return functools.partial(add_body, len(arrays)), list(arrays), [shape], []


def expand_body(count, picks, fan, cap, *refs):
    meta_refs, piece_refs = refs[:count], refs[count : count + fan]
    out_refs, held = refs[count + fan : -1], refs[-1]
    assemble(piece_refs, held)
    marks, _ = one_hots(meta_refs, picks, fan, cap, False)
    for mark, out_ref in zip(marks, out_refs):
        out_ref[...] = lax.dot_general(
            mark, held[...], ROWS, preferred_element_type=F32
        ).astype(out_ref.dtype)


def expanded(metas, pieces, picks, cap, dtypes):
    count, fan = len(metas), len(pieces)
    width = pieces[0].shape[1]
    return (
        functools.partial(expand_body, count, picks, fan, cap),
        [*metas, *pieces],
        [jax.ShapeDtypeStruct((width // META, width), d) for d in dtypes],
        [pltpu.VMEM((fan * pad16(count * cap), width), BF)],
    )


def tile_of(hidden):
    return 512 if hidden % 512 == 0 else 256


def forward_body(count, deps, *refs):
    piece_refs = refs[:count]
    gate_m, gate_o, linear_m, linear_o = refs[count : count + 4]
    x_ref, gate_factor_ref, linear_factor_ref, hidden_ref = refs[count + 4 + deps :]
    assemble(piece_refs, x_ref)
    half, hidden = gate_m.shape
    tile = tile_of(hidden)
    for start in range(0, hidden, tile):
        at = slice(start, start + tile)
        pre_gate = jnp.dot(x_ref[:, :half], gate_m[:, at], preferred_element_type=F32)
        pre_gate += jnp.dot(x_ref[:, half:], gate_o[:, at], preferred_element_type=F32)
        pre_linear = jnp.dot(x_ref[:, :half], linear_m[:, at], preferred_element_type=F32)
        pre_linear += jnp.dot(x_ref[:, half:], linear_o[:, at], preferred_element_type=F32)
        logistic = jax.nn.sigmoid(pre_gate)
        scaled = pre_gate * logistic
        hidden_ref[:, at] = (scaled * pre_linear).astype(BF)
        linear_factor_ref[:, at] = scaled.astype(BF)
        gate_factor_ref[:, at] = (
            pre_linear * logistic * (1.0 + pre_gate * (1.0 - logistic))
        ).astype(BF)


def forward(pieces, gate, linear, deps):
    count = len(pieces)
    size, width = pieces[0].shape
    rows = count * pad16(size)
    hidden = gate[0].shape[1]
    return pl.pallas_call(
        functools.partial(forward_body, count, len(deps)),
        in_specs=[VMEM] * (count + 4) + [ANY] * len(deps),
        out_specs=[VMEM] * 4,
        out_shape=[jax.ShapeDtypeStruct((rows, width), BF)]
        + [jax.ShapeDtypeStruct((rows, hidden), BF)] * 3,
        compiler_params=params(10),
        cost_estimate=cost(4 * rows * width * hidden, 6 * rows * hidden + 4 * width * hidden),
        name="forward_rows",
    )(*pieces, *gate, *linear, *deps)


def backward_body(count, deps, *refs):
    piece_refs = refs[:count]
    gate_factor, linear_factor, out_m, out_o = refs[count : count + 4]
    gate_m, gate_o, linear_m, linear_o = refs[count + 4 : count + 8]
    refs = refs[count + 8 + deps :]
    b_ref, gate_delta_ref, linear_delta_ref = refs[:3]
    row_refs, total = refs[3:-1], refs[-1]
    assemble(piece_refs, b_ref)
    hidden, half = out_m.shape
    tile = tile_of(hidden)
    for start in range(0, hidden, tile):
        at = slice(start, start + tile)
        grad = lax.dot_general(b_ref[:, :half], out_m[at, :], LAST, preferred_element_type=F32)
        grad += lax.dot_general(b_ref[:, half:], out_o[at, :], LAST, preferred_element_type=F32)
        gate_delta_ref[:, at] = (grad * gate_factor[:, at].astype(F32)).astype(BF)
        linear_delta_ref[:, at] = (grad * linear_factor[:, at].astype(F32)).astype(BF)
    for start, gate, linear in ((0, gate_m, linear_m), (half, gate_o, linear_o)):
        part = lax.dot_general(gate_delta_ref[...], gate[...], LAST, preferred_element_type=F32)
        part += lax.dot_general(
            linear_delta_ref[...], linear[...], LAST, preferred_element_type=F32
        )
        total[:, start : start + half] = part
    size = row_refs[0].shape[0]
    for i, ref in enumerate(row_refs):
        start = i * pad16(size)
        ref[...] = total[start : start + size, :].astype(BF)


def backward(pieces, gate_factor, linear_factor, out, gate, linear, deps):
    count = len(pieces)
    size, width = pieces[0].shape
    rows = count * pad16(size)
    hidden = gate_factor.shape[1]
    results = pl.pallas_call(
        functools.partial(backward_body, count, len(deps)),
        in_specs=[VMEM] * (count + 8) + [ANY] * len(deps),
        out_specs=[VMEM] * (3 + count),
        out_shape=[jax.ShapeDtypeStruct((rows, width), BF)]
        + [jax.ShapeDtypeStruct((rows, hidden), BF)] * 2
        + [jax.ShapeDtypeStruct((size, width), BF)] * count,
        scratch_shapes=[pltpu.VMEM((rows, width), F32)],
        compiler_params=params(10),
        cost_estimate=cost(6 * rows * width * hidden, 8 * rows * hidden + 6 * width * hidden),
        name="backward_rows",
    )(*pieces, gate_factor, linear_factor, *out, *gate, *linear, *deps)
    return results[:3], results[3:]


def weight_body(groups, column, deps, *refs):
    outs = refs[5 * groups + deps :]
    width, hidden = refs[0].shape[1], refs[2].shape[1]
    half, tile = width // 2, tile_of(hidden)
    side = slice(column * half, (column + 1) * half)
    for start in range(0, hidden, tile):
        at = slice(start, start + tile)
        totals = [None, None, None]
        for g in range(groups):
            x_ref, b_ref, gate_delta, linear_delta, hid = refs[5 * g : 5 * g + 5]
            for i, (a, b) in enumerate(
                (
                    (x_ref[:, side], gate_delta[:, at]),
                    (x_ref[:, side], linear_delta[:, at]),
                    (hid[:, at], b_ref[:, side]),
                )
            ):
                term = lax.dot_general(a, b, ROWS, preferred_element_type=F32)
                totals[i] = term if totals[i] is None else totals[i] + term
        outs[0][:half, at] = totals[0].astype(BF)
        outs[0][half:, at] = totals[1].astype(BF)
        outs[1][at, :] = totals[2].astype(BF)


def weight_grads(groups, column, deps):
    hidden = groups[0][2].shape[1]
    width = groups[0][0].shape[1]
    half = width // 2
    operands = [a for group in groups for a in group]
    total_rows = sum(group[0].shape[0] for group in groups)
    return pl.pallas_call(
        functools.partial(weight_body, len(groups), column, len(deps)),
        in_specs=[VMEM] * len(operands) + [ANY] * len(deps),
        out_specs=[VMEM] * 2,
        out_shape=[jax.ShapeDtypeStruct(s, BF) for s in ((width, hidden), (hidden, half))],
        compiler_params=params(12),
        cost_estimate=cost(
            3 * total_rows * width * hidden, 6 * total_rows * hidden + 3 * width * hidden
        ),
        name="weight_grads",
    )(*operands, *deps)


def split_body(mine_ref, theirs_ref, top_ref, bottom_ref):
    half = top_ref.shape[0]
    for out_ref, at in ((top_ref, slice(0, half)), (bottom_ref, slice(half, 2 * half))):
        out_ref[...] = (mine_ref[at, :].astype(F32) + theirs_ref[at, :].astype(F32)).astype(BF)


def added_halves(mine, theirs):
    rows, hidden = mine.shape
    return split_body, [mine, theirs], [jax.ShapeDtypeStruct((rows // 2, hidden), BF)] * 2, []


def finish_body(count, *refs):
    part_refs, (down_m, down_o), out_ref = refs[:count], refs[count : count + 2], refs[-1]
    total = part_refs[0][...].astype(F32)
    for ref in part_refs[1:]:
        total = total + ref[...].astype(F32)
    total = total.astype(BF)
    model, half = down_m.shape
    tile = tile_of(model)
    for start in range(0, model, tile):
        at = slice(start, start + tile)
        part = lax.dot_general(total[:, :half], down_m[at, :], LAST, preferred_element_type=F32)
        part += lax.dot_general(total[:, half:], down_o[at, :], LAST, preferred_element_type=F32)
        out_ref[:, at] = part.astype(BF)


def finish(parts, down, deps):
    tokens, model = parts[0].shape[0], down[0].shape[0]
    return pl.pallas_call(
        lambda *refs: finish_body(len(parts), *refs[: len(parts) + 2], refs[-1]),
        in_specs=[VMEM] * (len(parts) + 2) + [ANY] * len(deps),
        out_specs=VMEM,
        out_shape=jax.ShapeDtypeStruct((tokens, model), BF),
        compiler_params=params(10),
        cost_estimate=cost(2 * tokens * model * parts[0].shape[1], 4 * down[0].size),
        name="token_grad",
    )(*parts, *down, *deps)


def on_device(
    tokens,
    cotangent,
    expert_ids,
    slot_ids,
    gate_weights,
    latent_down,
    latent_up,
    expert_gate,
    expert_linear,
    expert_out,
):
    row_count = tokens.shape[0]
    pick_count = expert_ids.shape[1]
    group_count = lax.axis_size("expert")
    halves = lax.axis_size("half")
    expert_count = group_count * expert_gate.shape[0]
    capacity = min(
        row_count, 2 * ((9 * row_count * pick_count + 16 * expert_count - 1) // (16 * expert_count))
    )
    inner = group_count // PLANES
    fan = inner // SIDE

    def swap(a):
        return lax.ppermute(a, "dp", [(0, 1), (1, 0)])

    def along(a, shift):
        return lax.ppermute(
            a,
            "expert",
            [
                (z * inner + p, (z + shift) % PLANES * inner + p)
                for z in range(PLANES)
                for p in range(inner)
            ],
        )

    def beside(a):
        return lax.ppermute(a, "expert", [(i, i ^ 1) for i in range(group_count)])

    def across(parts):
        return [parts[0]] + [
            lax.ppermute(parts[k], "expert", [(i, i ^ (SIDE * k)) for i in range(group_count)])
            for k in range(1, fan)
        ]

    def summed(a):
        return lax.psum(a, "half") if halves > 1 else a

    last = []

    def deps(*extra):
        return [*last[-1:], *extra]

    def step(result):
        last.append(result[0] if isinstance(result, (list, tuple)) else result)
        return result

    def dot(a, weight, dims):
        if last:
            a = lax.optimization_barrier((a, last[-1]))[0]
        result = lax.dot_general(a, weight, dims, preferred_element_type=F32)
        return step(summed(result).astype(BF))

    def swapped_after(arrays, extra):
        held = lax.optimization_barrier((*arrays, *extra))[: len(arrays)]
        return [(a, swap(a)) for a in held]

    their_tokens, their_cotangent = swap(tokens), swap(cotangent)
    gate, linear, out = swapped_after(
        (expert_gate[0], expert_linear[0], expert_out[0]), (their_tokens,)
    )
    rows_first = (((1,), (0,)), ((), ()))
    latent_own = dot(tokens, latent_down, rows_first)
    latent_other = swap(dot(their_tokens, latent_down, rows_first))
    latent = step(
        join_rows(
            latent_own, latent_other, (expert_ids.T, slot_ids.T, gate_weights.T), deps()
        )
    )
    back_own = dot(cotangent, latent_up, LAST)
    back_other = swap(dot(their_cotangent, latent_up, LAST))

    blocks, pairs, pieces = {("l", 0): latent}, {}, {}

    def to_plane(kind, c, *extra):
        block = blocks[kind, 0]
        if extra:
            block = step(tie(block, deps(*extra)))
        with jax.named_scope(f"plane_{kind}{c}"):
            blocks[kind, c] = along(block, c)

    def to_side(kind, c, tied=False):
        if tied:
            blocks[kind, c] = step(tie(blocks[kind, c], deps()))
        with jax.named_scope(f"side_{kind}{c}"):
            pairs[kind, c] = [blocks[kind, c], beside(blocks[kind, c])]

    def pick(kind, c, *extra):
        parts = step(
            select(
                pairs["l", c], pairs[kind, c], pick_count, fan, capacity, kind == "b", deps(*extra)
            )
        )
        with jax.named_scope(f"piece_{kind}{c}"):
            pieces[kind, c] = across(parts)

    def come(kind, c):
        return pieces[kind, c][-1]

    factors, saved, rows, partial = {}, {}, {}, {}

    def ahead(chunks):
        factors[chunks] = step(
            forward([a for c in chunks for a in pieces["l", c]], gate, linear, deps())
        )

    def behind(chunks, *extra):
        x, gate_factor, linear_factor, hid = factors[chunks]
        (b, gate_delta, linear_delta), sums = backward(
            [a for c in chunks for a in pieces["b", c]],
            gate_factor,
            linear_factor,
            out,
            gate,
            linear,
            deps(*extra),
        )
        step(b)
        saved[chunks] = (x, b, gate_delta, linear_delta, hid)
        for i, c in enumerate(chunks):
            rows[c] = sums[i * fan : (i + 1) * fan]

    def send_rows(c, operands):
        with jax.named_scope(f"piece_r{c}"):
            rows[c] = across([rows[c][0], *operands])

    def send_side(c, results):
        own, other = results
        with jax.named_scope(f"side_r{c}"):
            partial[c] = [own, beside(other)]

    def send_home(c, results):
        with jax.named_scope(f"plane_r{c}"):
            partial[c] = along(results[0], -c)

    def turn(parts, through=(), extra=()):
        results, passed = bundle(parts, list(through), deps(*extra))
        step(results[0][0])
        return [*results, *passed]

    def gathered(c):
        return expanded(pairs["l", c], rows[c], pick_count, capacity, [F32, BF])

    to_plane("l", 1)
    to_side("l", 0)
    to_plane("l", 3, gate[1])
    back = step(join_rows(back_own, back_other, (), deps()))
    blocks["b", 0] = back
    pick("l", 0, blocks["l", 1], linear[1], out[1])
    to_side("l", 1)
    to_plane("l", 2, blocks["l", 1])
    pick("l", 1, blocks["l", 3])
    to_side("l", 3)
    to_plane("b", 2, blocks["l", 3])
    pick("l", 3, come("l", 0))
    to_side("b", 0)
    pick("b", 0, come("l", 1), blocks["l", 2])
    to_side("l", 2)
    to_plane("b", 3, blocks["l", 2])
    ahead((0, 1))
    pick("l", 2, come("l", 3), blocks["b", 2])
    to_side("b", 2)
    to_plane("b", 1, blocks["b", 2])
    (down,) = swapped_after((latent_down,), last[-1:])
    pick("b", 2, come("b", 0), blocks["b", 3])
    to_side("b", 3)
    ahead((3, 2))
    pick("b", 3, come("l", 2), blocks["b", 1])
    to_side("b", 1)
    pick("b", 1, come("b", 2), down[1])
    behind((3, 2))
    send_rows(3, rows[3][1:])
    behind((0, 1))
    results = turn([gathered(3), copies(rows[2][1:])])
    send_side(3, results[0])
    send_rows(2, results[1])
    theirs = weight_grads(list(saved.values()), 1, deps())
    step(theirs)
    results = turn([gathered(2), added(partial[3], BF), copies(rows[1][1:])], theirs)
    send_side(2, results[0])
    send_home(3, results[1])
    send_rows(1, results[2])
    received = [swap(results[3])]
    ours = weight_grads(list(saved.values()), 0, deps())
    step(ours)
    results = turn(
        [gathered(1), added(partial[2], BF), copies(rows[0][1:])],
        results[4:],
        [partial[3], received[0]],
    )
    send_side(1, results[0])
    send_home(2, results[1])
    send_rows(0, results[2])
    received.append(swap(results[3]))
    (grads,) = turn([added_halves(ours[0], received[0])])
    results = turn([gathered(0), added(partial[1], BF)], (), [received[1]])
    send_side(0, results[0])
    send_home(1, results[1])
    results = turn([added([ours[1], received[1]], BF)])
    grads = [*grads, results[0][0]]
    parts = [*partial[0], partial[1], partial[2], partial[3]]
    if halves > 1:
        results = turn([added(parts, F32)])
        parts = [summed(results[0][0])]
    token_grad = finish(parts, down, deps())
    return (token_grad, grads[0][None], grads[1][None], grads[2][None])


def solution(mesh):
    in_specs = (
        P(("expert", "dp"), "half"),
        P(("expert", "dp"), "half"),
        P(("expert", "dp"), None),
        P(("expert", "dp"), None),
        P(("expert", "dp"), None),
        P("half", "dp"),
        P("dp", "half"),
        P("expert", "dp", "half"),
        P("expert", "dp", "half"),
        P("expert", "half", "dp"),
    )
    out_specs = (
        P(("expert", "dp"), "half"),
        P("expert", "dp", "half"),
        P("expert", "dp", "half"),
        P("expert", "half", "dp"),
    )
    return jax.shard_map(
        on_device, mesh=mesh, in_specs=in_specs, out_specs=out_specs, check_vma=False
    )
```

```python
import functools

import jax
import jax.numpy as jnp
from jax import lax
from jax.experimental import pallas as pl
from jax.experimental.pallas import tpu as pltpu
from jax.sharding import PartitionSpec as P

BF = jnp.bfloat16
F32 = jnp.float32
PLANES = 4
SIDE = 2
META = 8
SIDE_TIE = True
SCALE = 1
MIB = 1024 * 1024
ROWS = (((0,), (0,)), ((), ()))
LAST = (((1,), (1,)), ((), ()))
ANY = pl.BlockSpec(memory_space=pl.ANY)
VMEM = pl.BlockSpec(memory_space=pltpu.VMEM)


def pad16(n):
    return (n + 15) // 16 * 16


def params(mib):
    return pltpu.CompilerParams(vmem_limit_bytes=mib * MIB)


def cost(flops, moved):
    return pl.CostEstimate(flops=int(flops * SCALE) + 1, bytes_accessed=int(moved * SCALE) + 1, transcendentals=0)


def whole(shape):
    return pl.BlockSpec(shape, lambda *_: (0,) * len(shape))


def join_body(routes, own_ref, other_ref, *refs):
    out_ref = refs[-1]
    tokens, half = own_ref.shape
    out_ref[:tokens, :half] = own_ref[...]
    out_ref[:tokens, half:] = other_ref[...]
    if routes:
        ids_ref, slots_ref, gates_ref = refs[:3]
        gates = gates_ref[...]
        high = gates.astype(BF)
        rest = gates - high.astype(F32)
        middle = rest.astype(BF)
        low = (rest - middle.astype(F32)).astype(BF)
        kinds = [ids_ref[...].astype(F32).astype(BF), slots_ref[...].astype(F32).astype(BF)]
        kinds += [high, middle, low]
        kinds += [jnp.zeros_like(low)] * (META - len(kinds))
        picks = gates.shape[0]
        table = jnp.concatenate([a.astype(F32) for a in kinds], axis=1)
        table = jnp.concatenate(
            [table, jnp.zeros((pad16(picks) - picks, table.shape[1]), F32)], axis=0
        )
        out_ref[tokens:, :] = table.astype(BF)


def join_rows(own, other, routes, deps):
    tokens, half = own.shape
    extra = pad16(routes[0].shape[0]) if routes else 0
    return pl.pallas_call(
        functools.partial(join_body, bool(routes)),
        out_shape=jax.ShapeDtypeStruct((tokens + extra, 2 * half), BF),
        in_specs=[VMEM] * (2 + len(routes)) + [ANY] * len(deps),
        out_specs=VMEM,
        compiler_params=params(8),
        cost_estimate=cost(0, 8 * tokens * half),
        name="join_rows",
    )(own, other, *routes, *deps)


def tie_body(block_ref, *refs):
    refs[-1][...] = block_ref[...]


def tie(block, deps):
    return pl.pallas_call(
        tie_body,
        out_shape=jax.ShapeDtypeStruct(block.shape, block.dtype),
        in_specs=[VMEM] + [ANY] * len(deps),
        out_specs=VMEM,
        compiler_params=params(8),
        cost_estimate=cost(0, 4 * block.size),
        name="tie_rows",
    )(block, *deps)


def one_hots(meta_refs, picks, fan, cap, weighted):
    me = lax.axis_index("expert")
    padded = pad16(len(meta_refs) * cap)
    marks, total = [], None
    for j, ref in enumerate(meta_refs):
        tokens = ref.shape[1] // META
        start = ref.shape[0] - pad16(picks)
        kinds = [
            ref[start:, i * tokens : (i + 1) * tokens].astype(F32)
            for i in range(5 if weighted else 2)
        ]
        held = kinds[0] * cap + kinds[1]
        row = lax.broadcasted_iota(jnp.int32, (padded, tokens), 0)
        inside = jnp.logical_and(row >= j * cap, row < (j + 1) * cap)
        targets = []
        for k in range(fan):
            base = lax.bitwise_xor(me, SIDE * k) * cap - j * cap
            targets.append(jnp.where(inside, row + base, -1))
        target = jnp.concatenate(targets, axis=0).astype(F32)
        mark = jnp.zeros(target.shape, F32)
        weight = jnp.zeros(target.shape, F32)
        if weighted:
            gate = kinds[2] + kinds[3] + kinds[4]
        for i in range(picks):
            equal = target == held[i : i + 1, :]
            mark = jnp.where(equal, 1.0, mark)
            if weighted:
                weight = jnp.where(equal, gate[i : i + 1, :], weight)
        marks.append(mark.astype(BF))
        if weighted:
            weight = jnp.sum(weight, axis=1, keepdims=True)
            total = weight if total is None else total + weight
    return marks, total


def select_body(count, picks, fan, cap, weighted, deps, *refs):
    meta_refs, block_refs, piece_refs = refs[:count], refs[count : 2 * count], refs[2 * count + deps :]
    marks, weight = one_hots(meta_refs, picks, fan, cap, weighted)
    tokens = marks[0].shape[1]
    rows = None
    for mark, block_ref in zip(marks, block_refs):
        term = jnp.dot(mark, block_ref[:tokens, :], preferred_element_type=F32)
        rows = term if rows is None else rows + term
    if weighted:
        rows = rows * weight
    padded = pad16(count * cap)
    for k in range(fan):
        piece_refs[k][...] = rows[k * padded : k * padded + count * cap, :].astype(BF)


def select(metas, blocks, picks, fan, cap, weighted, deps):
    count = len(blocks)
    width = blocks[0].shape[1]
    tokens = width // META
    return pl.pallas_call(
        functools.partial(select_body, count, picks, fan, cap, weighted, len(deps)),
        out_shape=[jax.ShapeDtypeStruct((count * cap, width), BF)] * fan,
        in_specs=[VMEM] * (2 * count) + [ANY] * len(deps),
        out_specs=[VMEM] * fan,
        compiler_params=params(10),
        cost_estimate=cost(
            2 * fan * count * count * cap * tokens * width, 8 * count * tokens * width
        ),
        name="select_back" if weighted else "select_latent",
    )(*metas, *blocks, *deps)


def assemble(piece_refs, out_ref):
    rows = piece_refs[0].shape[0]
    padded = pad16(rows)
    for i, ref in enumerate(piece_refs):
        if padded > rows:
            out_ref[(i + 1) * padded - 16 : (i + 1) * padded, :] = jnp.zeros(
                (16, out_ref.shape[1]), out_ref.dtype
            )
        out_ref[i * padded : i * padded + rows, :] = ref[...]


def bundle_body(parts, held_over, deps, *refs):
    at = sum(len(part[1]) for part in parts)
    ins, refs = refs[:at], refs[at + held_over + deps :]
    outs_count = sum(len(part[2]) for part in parts)
    outs, scratch = refs[:outs_count], refs[outs_count + held_over :]
    for body, operands, results, held in parts:
        body(*ins[: len(operands)], *outs[: len(results)], *scratch[: len(held)])
        ins, outs, scratch = ins[len(operands) :], outs[len(results) :], scratch[len(held) :]


def bundle(parts, through, deps):
    operands = [a for part in parts for a in part[1]]
    shapes = [a for part in parts for a in part[2]]
    sizes = sum(a.size for a in operands)
    results = pl.pallas_call(
        functools.partial(bundle_body, parts, len(through), len(deps)),
        out_shape=shapes + [jax.ShapeDtypeStruct(a.shape, a.dtype) for a in through],
        in_specs=[VMEM] * len(operands) + [ANY] * (len(through) + len(deps)),
        out_specs=[VMEM] * len(shapes) + [ANY] * len(through),
        input_output_aliases={len(operands) + i: len(shapes) + i for i in range(len(through))},
        scratch_shapes=[a for part in parts for a in part[3]],
        compiler_params=params(10),
        cost_estimate=cost(0, 4 * sizes),
        name="return_rows",
    )(*operands, *through, *deps)
    split = []
    for part in parts:
        split.append(results[: len(part[2])])
        results = results[len(part[2]) :]
    return split, results


def copy_body(count, *refs):
    for i in range(count):
        refs[count + i][...] = refs[i][...]


def copies(arrays):
    shapes = [jax.ShapeDtypeStruct(a.shape, a.dtype) for a in arrays]
    return functools.partial(copy_body, len(arrays)), list(arrays), shapes, []


def add_body(count, *refs):
    total = refs[0][...].astype(F32)
    for ref in refs[1:count]:
        total = total + ref[...].astype(F32)
    refs[count][...] = total.astype(refs[count].dtype)


def added(arrays, dtype):
    shape = jax.ShapeDtypeStruct(arrays[0].shape, dtype)
    return functools.partial(add_body, len(arrays)), list(arrays), [shape], []


def expand_body(count, picks, fan, cap, *refs):
    meta_refs, piece_refs = refs[:count], refs[count : count + fan]
    out_refs, held = refs[count + fan : -1], refs[-1]
    assemble(piece_refs, held)
    marks, _ = one_hots(meta_refs, picks, fan, cap, False)
    for mark, out_ref in zip(marks, out_refs):
        out_ref[...] = lax.dot_general(
            mark, held[...], ROWS, preferred_element_type=F32
        ).astype(out_ref.dtype)


def expanded(metas, pieces, picks, cap, dtypes):
    count, fan = len(metas), len(pieces)
    width = pieces[0].shape[1]
    return (
        functools.partial(expand_body, count, picks, fan, cap),
        [*metas, *pieces],
        [jax.ShapeDtypeStruct((width // META, width), d) for d in dtypes],
        [pltpu.VMEM((fan * pad16(count * cap), width), BF)],
    )


def tile_of(hidden):
    return 512 if hidden % 512 == 0 else 256


def forward_body(count, deps, *refs):
    piece_refs = refs[:count]
    gate_m, gate_o, linear_m, linear_o = refs[count : count + 4]
    x_ref, gate_factor_ref, linear_factor_ref, hidden_ref = refs[count + 4 + deps :]
    assemble(piece_refs, x_ref)
    half, hidden = gate_m.shape
    tile = tile_of(hidden)
    @pl.loop(0, hidden // tile)
    def _(j):
        at = pl.ds(pl.multiple_of(j * tile, tile), tile)
        pre_gate = jnp.dot(x_ref[:, :half], gate_m[:, at], preferred_element_type=F32)
        pre_gate += jnp.dot(x_ref[:, half:], gate_o[:, at], preferred_element_type=F32)
        pre_linear = jnp.dot(x_ref[:, :half], linear_m[:, at], preferred_element_type=F32)
        pre_linear += jnp.dot(x_ref[:, half:], linear_o[:, at], preferred_element_type=F32)
        logistic = jax.nn.sigmoid(pre_gate)
        scaled = pre_gate * logistic
        hidden_ref[:, at] = (scaled * pre_linear).astype(BF)
        linear_factor_ref[:, at] = scaled.astype(BF)
        gate_factor_ref[:, at] = (
            pre_linear * logistic * (1.0 + pre_gate * (1.0 - logistic))
        ).astype(BF)


def forward(pieces, gate, linear, deps):
    count = len(pieces)
    size, width = pieces[0].shape
    rows = count * pad16(size)
    hidden = gate[0].shape[1]
    return pl.pallas_call(
        functools.partial(forward_body, count, len(deps)),
        in_specs=[VMEM] * (count + 4) + [ANY] * len(deps),
        out_specs=[VMEM] * 4,
        out_shape=[jax.ShapeDtypeStruct((rows, width), BF)]
        + [jax.ShapeDtypeStruct((rows, hidden), BF)] * 3,
        compiler_params=params(10),
        cost_estimate=cost(4 * rows * width * hidden, 6 * rows * hidden + 4 * width * hidden),
        name="forward_rows",
    )(*pieces, *gate, *linear, *deps)


def backward_body(count, deps, *refs):
    piece_refs = refs[:count]
    gate_factor, linear_factor, out_m, out_o = refs[count : count + 4]
    gate_m, gate_o, linear_m, linear_o = refs[count + 4 : count + 8]
    refs = refs[count + 8 + deps :]
    b_ref, gate_delta_ref, linear_delta_ref = refs[:3]
    row_refs, total = refs[3:-1], refs[-1]
    assemble(piece_refs, b_ref)
    hidden, half = out_m.shape
    tile = tile_of(hidden)
    for start in range(0, hidden, tile):
        at = slice(start, start + tile)
        grad = lax.dot_general(b_ref[:, :half], out_m[at, :], LAST, preferred_element_type=F32)
        grad += lax.dot_general(b_ref[:, half:], out_o[at, :], LAST, preferred_element_type=F32)
        gate_delta_ref[:, at] = (grad * gate_factor[:, at].astype(F32)).astype(BF)
        linear_delta_ref[:, at] = (grad * linear_factor[:, at].astype(F32)).astype(BF)
    for start, gate, linear in ((0, gate_m, linear_m), (half, gate_o, linear_o)):
        part = lax.dot_general(gate_delta_ref[...], gate[...], LAST, preferred_element_type=F32)
        part += lax.dot_general(
            linear_delta_ref[...], linear[...], LAST, preferred_element_type=F32
        )
        total[:, start : start + half] = part
    size = row_refs[0].shape[0]
    for i, ref in enumerate(row_refs):
        start = i * pad16(size)
        ref[...] = total[start : start + size, :].astype(BF)


def backward(pieces, gate_factor, linear_factor, out, gate, linear, deps):
    count = len(pieces)
    size, width = pieces[0].shape
    rows = count * pad16(size)
    hidden = gate_factor.shape[1]
    results = pl.pallas_call(
        functools.partial(backward_body, count, len(deps)),
        in_specs=[VMEM] * (count + 8) + [ANY] * len(deps),
        out_specs=[VMEM] * (3 + count),
        out_shape=[jax.ShapeDtypeStruct((rows, width), BF)]
        + [jax.ShapeDtypeStruct((rows, hidden), BF)] * 2
        + [jax.ShapeDtypeStruct((size, width), BF)] * count,
        scratch_shapes=[pltpu.VMEM((rows, width), F32)],
        compiler_params=params(10),
        cost_estimate=cost(6 * rows * width * hidden, 8 * rows * hidden + 6 * width * hidden),
        name="backward_rows",
    )(*pieces, gate_factor, linear_factor, *out, *gate, *linear, *deps)
    return results[:3], results[3:]


def weight_body(groups, column, deps, *refs):
    outs = refs[5 * groups + deps :]
    width, hidden = refs[0].shape[1], refs[2].shape[1]
    half, tile = width // 2, tile_of(hidden)
    side = slice(column * half, (column + 1) * half)
    @pl.loop(0, hidden // tile)
    def _(j):
        at = pl.ds(pl.multiple_of(j * tile, tile), tile)
        totals = [None, None, None]
        for g in range(groups):
            x_ref, b_ref, gate_delta, linear_delta, hid = refs[5 * g : 5 * g + 5]
            for i, (a, b) in enumerate(
                (
                    (x_ref[:, side], gate_delta[:, at]),
                    (x_ref[:, side], linear_delta[:, at]),
                    (hid[:, at], b_ref[:, side]),
                )
            ):
                term = lax.dot_general(a, b, ROWS, preferred_element_type=F32)
                totals[i] = term if totals[i] is None else totals[i] + term
        outs[0][:half, at] = totals[0].astype(BF)
        outs[0][half:, at] = totals[1].astype(BF)
        outs[1][at, :] = totals[2].astype(BF)


def weight_grads(groups, column, deps):
    hidden = groups[0][2].shape[1]
    width = groups[0][0].shape[1]
    half = width // 2
    operands = [a for group in groups for a in group]
    total_rows = sum(group[0].shape[0] for group in groups)
    return pl.pallas_call(
        functools.partial(weight_body, len(groups), column, len(deps)),
        in_specs=[VMEM] * len(operands) + [ANY] * len(deps),
        out_specs=[VMEM] * 2,
        out_shape=[jax.ShapeDtypeStruct(s, BF) for s in ((width, hidden), (hidden, half))],
        compiler_params=params(12),
        cost_estimate=cost(
            3 * total_rows * width * hidden, 6 * total_rows * hidden + 3 * width * hidden
        ),
        name="weight_grads",
    )(*operands, *deps)


def split_body(mine_ref, theirs_ref, top_ref, bottom_ref):
    half = top_ref.shape[0]
    for out_ref, at in ((top_ref, slice(0, half)), (bottom_ref, slice(half, 2 * half))):
        out_ref[...] = (mine_ref[at, :].astype(F32) + theirs_ref[at, :].astype(F32)).astype(BF)


def added_halves(mine, theirs):
    rows, hidden = mine.shape
    return split_body, [mine, theirs], [jax.ShapeDtypeStruct((rows // 2, hidden), BF)] * 2, []


def finish_body(count, *refs):
    part_refs, (down_m, down_o), out_ref = refs[:count], refs[count : count + 2], refs[-1]
    total = part_refs[0][...].astype(F32)
    for ref in part_refs[1:]:
        total = total + ref[...].astype(F32)
    total = total.astype(BF)
    model, half = down_m.shape
    tile = tile_of(model)
    for start in range(0, model, tile):
        at = slice(start, start + tile)
        part = lax.dot_general(total[:, :half], down_m[at, :], LAST, preferred_element_type=F32)
        part += lax.dot_general(total[:, half:], down_o[at, :], LAST, preferred_element_type=F32)
        out_ref[:, at] = part.astype(BF)


def finish(parts, down, deps):
    tokens, model = parts[0].shape[0], down[0].shape[0]
    return pl.pallas_call(
        lambda *refs: finish_body(len(parts), *refs[: len(parts) + 2], refs[-1]),
        in_specs=[VMEM] * (len(parts) + 2) + [ANY] * len(deps),
        out_specs=VMEM,
        out_shape=jax.ShapeDtypeStruct((tokens, model), BF),
        compiler_params=params(10),
        cost_estimate=cost(2 * tokens * model * parts[0].shape[1], 4 * down[0].size),
        name="token_grad",
    )(*parts, *down, *deps)


def on_device(
    tokens,
    cotangent,
    expert_ids,
    slot_ids,
    gate_weights,
    latent_down,
    latent_up,
    expert_gate,
    expert_linear,
    expert_out,
):
    row_count = tokens.shape[0]
    pick_count = expert_ids.shape[1]
    group_count = lax.axis_size("expert")
    halves = lax.axis_size("half")
    expert_count = group_count * expert_gate.shape[0]
    capacity = min(
        row_count, 2 * ((9 * row_count * pick_count + 16 * expert_count - 1) // (16 * expert_count))
    )
    inner = group_count // PLANES
    fan = inner // SIDE

    def swap(a):
        return lax.ppermute(a, "dp", [(0, 1), (1, 0)])

    def along(a, shift):
        return lax.ppermute(
            a,
            "expert",
            [
                (z * inner + p, (z + shift) % PLANES * inner + p)
                for z in range(PLANES)
                for p in range(inner)
            ],
        )

    def beside(a):
        return lax.ppermute(a, "expert", [(i, i ^ 1) for i in range(group_count)])

    def across(parts):
        return [parts[0]] + [
            lax.ppermute(parts[k], "expert", [(i, i ^ (SIDE * k)) for i in range(group_count)])
            for k in range(1, fan)
        ]

    def summed(a):
        return lax.psum(a, "half") if halves > 1 else a

    last = []

    def deps(*extra):
        return [*last[-1:], *extra]

    def step(result):
        last.append(result[0] if isinstance(result, (list, tuple)) else result)
        return result

    def dot(a, weight, dims):
        if last:
            a = lax.optimization_barrier((a, last[-1]))[0]
        result = lax.dot_general(a, weight, dims, preferred_element_type=F32)
        return step(summed(result).astype(BF))

    def swapped_after(arrays, extra):
        held = lax.optimization_barrier((*arrays, *extra))[: len(arrays)]
        return [(a, swap(a)) for a in held]

    their_tokens, their_cotangent = swap(tokens), swap(cotangent)
    rows_first = (((1,), (0,)), ((), ()))
    latent_own = dot(tokens, latent_down, rows_first)
    latent_other = swap(dot(their_tokens, latent_down, rows_first))
    latent = step(
        join_rows(
            latent_own, latent_other, (expert_ids.T, slot_ids.T, gate_weights.T), deps()
        )
    )
    gate, linear, out = swapped_after(
        (expert_gate[0], expert_linear[0], expert_out[0]), (latent,)
    )
    back_own = dot(cotangent, latent_up, LAST)
    back_other = swap(dot(their_cotangent, latent_up, LAST))

    blocks, pairs, pieces = {("l", 0): latent}, {}, {}

    def to_plane(kind, c, *extra):
        block = blocks[kind, 0]
        if extra:
            block = step(tie(block, deps(*extra)))
        with jax.named_scope(f"plane_{kind}{c}"):
            blocks[kind, c] = along(block, c)

    def to_side(kind, c, tied=False):
        if tied:
            blocks[kind, c] = step(tie(blocks[kind, c], deps()))
        with jax.named_scope(f"side_{kind}{c}"):
            pairs[kind, c] = [blocks[kind, c], beside(blocks[kind, c])]

    def pick(kind, c, *extra):
        parts = step(
            select(
                pairs["l", c], pairs[kind, c], pick_count, fan, capacity, kind == "b", deps(*extra)
            )
        )
        with jax.named_scope(f"piece_{kind}{c}"):
            pieces[kind, c] = across(parts)

    def come(kind, c):
        return pieces[kind, c][-1]

    factors, saved, rows, partial = {}, {}, {}, {}

    def ahead(chunks):
        factors[chunks] = step(
            forward([a for c in chunks for a in pieces["l", c]], gate, linear, deps())
        )

    def behind(chunks, *extra):
        x, gate_factor, linear_factor, hid = factors[chunks]
        (b, gate_delta, linear_delta), sums = backward(
            [a for c in chunks for a in pieces["b", c]],
            gate_factor,
            linear_factor,
            out,
            gate,
            linear,
            deps(*extra),
        )
        step(b)
        saved[chunks] = (x, b, gate_delta, linear_delta, hid)
        for i, c in enumerate(chunks):
            rows[c] = sums[i * fan : (i + 1) * fan]

    def send_rows(c, operands):
        with jax.named_scope(f"piece_r{c}"):
            rows[c] = across([rows[c][0], *operands])

    def send_side(c, results):
        own, other = results
        with jax.named_scope(f"side_r{c}"):
            partial[c] = [own, beside(other)]

    def send_home(c, results):
        with jax.named_scope(f"plane_r{c}"):
            partial[c] = along(results[0], -c)

    def turn(parts, through=(), extra=()):
        results, passed = bundle(parts, list(through), deps(*extra))
        step(results[0][0])
        return [*results, *passed]

    def gathered(c):
        return expanded(pairs["l", c], rows[c], pick_count, capacity, [F32, BF])

    to_plane("l", 1)
    to_side("l", 0)
    to_plane("l", 3, gate[1])
    back = step(join_rows(back_own, back_other, (), deps()))
    blocks["b", 0] = back
    pick("l", 0, blocks["l", 1], linear[1], out[1])
    to_side("l", 1)
    to_plane("l", 2, blocks["l", 1])
    pick("l", 1, blocks["l", 3])
    to_side("l", 3)
    to_plane("b", 2, blocks["l", 3])
    pick("l", 3, come("l", 0))
    to_side("b", 0)
    pick("b", 0, come("l", 1), blocks["l", 2])
    to_side("l", 2)
    to_plane("b", 3, blocks["l", 2])
    ahead((0, 1))
    pick("l", 2, come("l", 3), blocks["b", 2])
    to_side("b", 2)
    to_plane("b", 1, blocks["b", 2])
    (down,) = swapped_after((latent_down,), last[-1:])
    pick("b", 2, come("b", 0), blocks["b", 3])
    to_side("b", 3)
    ahead((3, 2))
    pick("b", 3, come("l", 2), blocks["b", 1])
    to_side("b", 1)
    pick("b", 1, come("b", 2), down[1])
    behind((3, 2))
    send_rows(3, rows[3][1:])
    behind((0, 1))
    results = turn([gathered(3), copies(rows[2][1:])])
    send_side(3, results[0])
    send_rows(2, results[1])
    theirs = weight_grads(list(saved.values()), 1, deps())
    step(theirs)
    results = turn([gathered(2), added(partial[3], BF), copies(rows[1][1:])], theirs)
    send_side(2, results[0])
    send_home(3, results[1])
    send_rows(1, results[2])
    received = [swap(results[3])]
    ours = weight_grads(list(saved.values()), 0, deps())
    step(ours)
    results = turn(
        [gathered(1), added(partial[2], BF), copies(rows[0][1:])],
        results[4:],
        [partial[3], received[0]],
    )
    send_side(1, results[0])
    send_home(2, results[1])
    send_rows(0, results[2])
    received.append(swap(results[3]))
    (grads,) = turn([added_halves(ours[0], received[0])])
    results = turn([gathered(0), added(partial[1], BF)], (), [received[1]])
    send_side(0, results[0])
    send_home(1, results[1])
    results = turn([added([ours[1], received[1]], BF)])
    grads = [*grads, results[0][0]]
    parts = [*partial[0], partial[1], partial[2], partial[3]]
    if halves > 1:
        results = turn([added(parts, F32)])
        parts = [summed(results[0][0])]
    token_grad = finish(parts, down, deps())
    return (token_grad, grads[0][None], grads[1][None], grads[2][None])


def solution(mesh):
    in_specs = (
        P(("expert", "dp"), "half"),
        P(("expert", "dp"), "half"),
        P(("expert", "dp"), None),
        P(("expert", "dp"), None),
        P(("expert", "dp"), None),
        P("half", "dp"),
        P("dp", "half"),
        P("expert", "dp", "half"),
        P("expert", "dp", "half"),
        P("expert", "half", "dp"),
    )
    out_specs = (
        P(("expert", "dp"), "half"),
        P("expert", "dp", "half"),
        P("expert", "dp", "half"),
        P("expert", "half", "dp"),
    )
    return jax.shard_map(
        on_device, mesh=mesh, in_specs=in_specs, out_specs=out_specs, check_vma=False
    )
```

```python
import functools

import jax
import jax.numpy as jnp
from jax import lax
from jax.experimental import pallas as pl
from jax.experimental.pallas import tpu as pltpu
from jax.sharding import PartitionSpec as P

BF = jnp.bfloat16
F32 = jnp.float32
PLANES = 4
SIDE = 2
META = 8
SIDE_TIE = True
SCALE = 1
MIB = 1024 * 1024
ROWS = (((0,), (0,)), ((), ()))
LAST = (((1,), (1,)), ((), ()))
ANY = pl.BlockSpec(memory_space=pl.ANY)
VMEM = pl.BlockSpec(memory_space=pltpu.VMEM)


def pad16(n):
    return (n + 15) // 16 * 16


def params(mib):
    return pltpu.CompilerParams(vmem_limit_bytes=mib * MIB)


def cost(flops, moved):
    return pl.CostEstimate(flops=int(flops * SCALE) + 1, bytes_accessed=int(moved * SCALE) + 1, transcendentals=0)


def whole(shape):
    return pl.BlockSpec(shape, lambda *_: (0,) * len(shape))


def join_body(routes, own_ref, other_ref, *refs):
    out_ref = refs[-1]
    tokens, half = own_ref.shape
    out_ref[:tokens, :half] = own_ref[...]
    out_ref[:tokens, half:] = other_ref[...]
    if routes:
        ids_ref, slots_ref, gates_ref = refs[:3]
        gates = gates_ref[...]
        high = gates.astype(BF)
        rest = gates - high.astype(F32)
        middle = rest.astype(BF)
        low = (rest - middle.astype(F32)).astype(BF)
        kinds = [ids_ref[...].astype(F32).astype(BF), slots_ref[...].astype(F32).astype(BF)]
        kinds += [high, middle, low]
        kinds += [jnp.zeros_like(low)] * (META - len(kinds))
        picks = gates.shape[0]
        table = jnp.concatenate([a.astype(F32) for a in kinds], axis=1)
        table = jnp.concatenate(
            [table, jnp.zeros((pad16(picks) - picks, table.shape[1]), F32)], axis=0
        )
        out_ref[tokens:, :] = table.astype(BF)


def join_rows(own, other, routes, deps):
    tokens, half = own.shape
    extra = pad16(routes[0].shape[0]) if routes else 0
    return pl.pallas_call(
        functools.partial(join_body, bool(routes)),
        out_shape=jax.ShapeDtypeStruct((tokens + extra, 2 * half), BF),
        in_specs=[VMEM] * (2 + len(routes)) + [ANY] * len(deps),
        out_specs=VMEM,
        compiler_params=params(8),
        cost_estimate=cost(0, 8 * tokens * half),
        name="join_rows",
    )(own, other, *routes, *deps)


def tie_body(block_ref, *refs):
    refs[-1][...] = block_ref[...]


def tie(block, deps):
    return pl.pallas_call(
        tie_body,
        out_shape=jax.ShapeDtypeStruct(block.shape, block.dtype),
        in_specs=[VMEM] + [ANY] * len(deps),
        out_specs=VMEM,
        compiler_params=params(8),
        cost_estimate=cost(0, 4 * block.size),
        name="tie_rows",
    )(block, *deps)


def one_hots(meta_refs, picks, fan, cap, weighted):
    me = lax.axis_index("expert")
    padded = pad16(len(meta_refs) * cap)
    marks, total = [], None
    for j, ref in enumerate(meta_refs):
        tokens = ref.shape[1] // META
        start = ref.shape[0] - pad16(picks)
        kinds = [
            ref[start:, i * tokens : (i + 1) * tokens].astype(F32)
            for i in range(5 if weighted else 2)
        ]
        held = kinds[0] * cap + kinds[1]
        row = lax.broadcasted_iota(jnp.int32, (padded, tokens), 0)
        inside = jnp.logical_and(row >= j * cap, row < (j + 1) * cap)
        targets = []
        for k in range(fan):
            base = lax.bitwise_xor(me, SIDE * k) * cap - j * cap
            targets.append(jnp.where(inside, row + base, -1))
        target = jnp.concatenate(targets, axis=0).astype(F32)
        mark = jnp.zeros(target.shape, F32)
        weight = jnp.zeros(target.shape, F32)
        if weighted:
            gate = kinds[2] + kinds[3] + kinds[4]
        for i in range(picks):
            equal = target == held[i : i + 1, :]
            mark = jnp.where(equal, 1.0, mark)
            if weighted:
                weight = jnp.where(equal, gate[i : i + 1, :], weight)
        marks.append(mark.astype(BF))
        if weighted:
            weight = jnp.sum(weight, axis=1, keepdims=True)
            total = weight if total is None else total + weight
    return marks, total


def select_body(count, picks, fan, cap, weighted, deps, *refs):
    meta_refs, block_refs, piece_refs = refs[:count], refs[count : 2 * count], refs[2 * count + deps :]
    marks, weight = one_hots(meta_refs, picks, fan, cap, weighted)
    tokens = marks[0].shape[1]
    rows = None
    for mark, block_ref in zip(marks, block_refs):
        term = jnp.dot(mark, block_ref[:tokens, :], preferred_element_type=F32)
        rows = term if rows is None else rows + term
    if weighted:
        rows = rows * weight
    padded = pad16(count * cap)
    for k in range(fan):
        piece_refs[k][...] = rows[k * padded : k * padded + count * cap, :].astype(BF)


def select(metas, blocks, picks, fan, cap, weighted, deps):
    count = len(blocks)
    width = blocks[0].shape[1]
    tokens = width // META
    return pl.pallas_call(
        functools.partial(select_body, count, picks, fan, cap, weighted, len(deps)),
        out_shape=[jax.ShapeDtypeStruct((count * cap, width), BF)] * fan,
        in_specs=[VMEM] * (2 * count) + [ANY] * len(deps),
        out_specs=[VMEM] * fan,
        compiler_params=params(10),
        cost_estimate=cost(
            2 * fan * count * count * cap * tokens * width, 8 * count * tokens * width
        ),
        name="select_back" if weighted else "select_latent",
    )(*metas, *blocks, *deps)


def assemble(piece_refs, out_ref):
    rows = piece_refs[0].shape[0]
    padded = pad16(rows)
    for i, ref in enumerate(piece_refs):
        if padded > rows:
            out_ref[(i + 1) * padded - 16 : (i + 1) * padded, :] = jnp.zeros(
                (16, out_ref.shape[1]), out_ref.dtype
            )
        out_ref[i * padded : i * padded + rows, :] = ref[...]


def bundle_body(parts, held_over, deps, *refs):
    at = sum(len(part[1]) for part in parts)
    ins, refs = refs[:at], refs[at + held_over + deps :]
    outs_count = sum(len(part[2]) for part in parts)
    outs, scratch = refs[:outs_count], refs[outs_count + held_over :]
    for body, operands, results, held in parts:
        body(*ins[: len(operands)], *outs[: len(results)], *scratch[: len(held)])
        ins, outs, scratch = ins[len(operands) :], outs[len(results) :], scratch[len(held) :]


def bundle(parts, through, deps):
    operands = [a for part in parts for a in part[1]]
    shapes = [a for part in parts for a in part[2]]
    sizes = sum(a.size for a in operands)
    results = pl.pallas_call(
        functools.partial(bundle_body, parts, len(through), len(deps)),
        out_shape=shapes + [jax.ShapeDtypeStruct(a.shape, a.dtype) for a in through],
        in_specs=[VMEM] * len(operands) + [ANY] * (len(through) + len(deps)),
        out_specs=[VMEM] * len(shapes) + [ANY] * len(through),
        input_output_aliases={len(operands) + i: len(shapes) + i for i in range(len(through))},
        scratch_shapes=[a for part in parts for a in part[3]],
        compiler_params=params(10),
        cost_estimate=cost(0, 4 * sizes),
        name="return_rows",
    )(*operands, *through, *deps)
    split = []
    for part in parts:
        split.append(results[: len(part[2])])
        results = results[len(part[2]) :]
    return split, results


def copy_body(count, *refs):
    for i in range(count):
        refs[count + i][...] = refs[i][...]


def copies(arrays):
    shapes = [jax.ShapeDtypeStruct(a.shape, a.dtype) for a in arrays]
    return functools.partial(copy_body, len(arrays)), list(arrays), shapes, []


def mark_body(mark_ref):
    mark_ref[...] = jnp.zeros_like(mark_ref)


MARK = (mark_body, [], [jax.ShapeDtypeStruct((8, 128), F32)], [])


def add_body(count, *refs):
    total = refs[0][...].astype(F32)
    for ref in refs[1:count]:
        total = total + ref[...].astype(F32)
    refs[count][...] = total.astype(refs[count].dtype)


def added(arrays, dtype):
    shape = jax.ShapeDtypeStruct(arrays[0].shape, dtype)
    return functools.partial(add_body, len(arrays)), list(arrays), [shape], []


def expand_body(count, picks, fan, cap, *refs):
    meta_refs, piece_refs = refs[:count], refs[count : count + fan]
    out_refs, held = refs[count + fan : -1], refs[-1]
    assemble(piece_refs, held)
    marks, _ = one_hots(meta_refs, picks, fan, cap, False)
    for mark, out_ref in zip(marks, out_refs):
        out_ref[...] = lax.dot_general(
            mark, held[...], ROWS, preferred_element_type=F32
        ).astype(out_ref.dtype)


def expanded(metas, pieces, picks, cap, dtypes):
    count, fan = len(metas), len(pieces)
    width = pieces[0].shape[1]
    return (
        functools.partial(expand_body, count, picks, fan, cap),
        [*metas, *pieces],
        [jax.ShapeDtypeStruct((width // META, width), d) for d in dtypes],
        [pltpu.VMEM((fan * pad16(count * cap), width), BF)],
    )


def tile_of(hidden):
    return 512 if hidden % 512 == 0 else 256


def forward_body(count, deps, *refs):
    piece_refs = refs[:count]
    gate_m, gate_o, linear_m, linear_o = refs[count : count + 4]
    x_ref, gate_factor_ref, linear_factor_ref, hidden_ref, mark_ref = refs[count + 4 + deps :]
    mark_body(mark_ref)
    assemble(piece_refs, x_ref)
    half, hidden = gate_m.shape
    tile = tile_of(hidden)
    @pl.loop(0, hidden // tile)
    def _(j):
        at = pl.ds(pl.multiple_of(j * tile, tile), tile)
        pre_gate = jnp.dot(x_ref[:, :half], gate_m[:, at], preferred_element_type=F32)
        pre_gate += jnp.dot(x_ref[:, half:], gate_o[:, at], preferred_element_type=F32)
        pre_linear = jnp.dot(x_ref[:, :half], linear_m[:, at], preferred_element_type=F32)
        pre_linear += jnp.dot(x_ref[:, half:], linear_o[:, at], preferred_element_type=F32)
        logistic = jax.nn.sigmoid(pre_gate)
        scaled = pre_gate * logistic
        hidden_ref[:, at] = (scaled * pre_linear).astype(BF)
        linear_factor_ref[:, at] = scaled.astype(BF)
        gate_factor_ref[:, at] = (
            pre_linear * logistic * (1.0 + pre_gate * (1.0 - logistic))
        ).astype(BF)


def forward(pieces, gate, linear, deps):
    count = len(pieces)
    size, width = pieces[0].shape
    rows = count * pad16(size)
    hidden = gate[0].shape[1]
    return pl.pallas_call(
        functools.partial(forward_body, count, len(deps)),
        in_specs=[VMEM] * (count + 4) + [ANY] * len(deps),
        out_specs=[VMEM] * 5,
        out_shape=[jax.ShapeDtypeStruct((rows, width), BF)]
        + [jax.ShapeDtypeStruct((rows, hidden), BF)] * 3
        + [jax.ShapeDtypeStruct((8, 128), F32)],
        compiler_params=params(10),
        cost_estimate=cost(4 * rows * width * hidden, 6 * rows * hidden + 4 * width * hidden),
        name="forward_rows",
    )(*pieces, *gate, *linear, *deps)


def backward_body(count, deps, *refs):
    piece_refs = refs[:count]
    gate_factor, linear_factor, out_m, out_o = refs[count : count + 4]
    gate_m, gate_o, linear_m, linear_o = refs[count + 4 : count + 8]
    refs = refs[count + 8 + deps :]
    b_ref, gate_delta_ref, linear_delta_ref = refs[:3]
    row_refs, mark_ref, total = refs[3:-2], refs[-2], refs[-1]
    mark_body(mark_ref)
    assemble(piece_refs, b_ref)
    hidden, half = out_m.shape
    tile = tile_of(hidden)
    for start in range(0, hidden, tile):
        at = slice(start, start + tile)
        grad = lax.dot_general(b_ref[:, :half], out_m[at, :], LAST, preferred_element_type=F32)
        grad += lax.dot_general(b_ref[:, half:], out_o[at, :], LAST, preferred_element_type=F32)
        gate_delta_ref[:, at] = (grad * gate_factor[:, at].astype(F32)).astype(BF)
        linear_delta_ref[:, at] = (grad * linear_factor[:, at].astype(F32)).astype(BF)
    for start, gate, linear in ((0, gate_m, linear_m), (half, gate_o, linear_o)):
        part = lax.dot_general(gate_delta_ref[...], gate[...], LAST, preferred_element_type=F32)
        part += lax.dot_general(
            linear_delta_ref[...], linear[...], LAST, preferred_element_type=F32
        )
        total[:, start : start + half] = part
    size = row_refs[0].shape[0]
    for i, ref in enumerate(row_refs):
        start = i * pad16(size)
        ref[...] = total[start : start + size, :].astype(BF)


def backward(pieces, gate_factor, linear_factor, out, gate, linear, deps):
    count = len(pieces)
    size, width = pieces[0].shape
    rows = count * pad16(size)
    hidden = gate_factor.shape[1]
    results = pl.pallas_call(
        functools.partial(backward_body, count, len(deps)),
        in_specs=[VMEM] * (count + 8) + [ANY] * len(deps),
        out_specs=[VMEM] * (4 + count),
        out_shape=[jax.ShapeDtypeStruct((rows, width), BF)]
        + [jax.ShapeDtypeStruct((rows, hidden), BF)] * 2
        + [jax.ShapeDtypeStruct((size, width), BF)] * count
        + [jax.ShapeDtypeStruct((8, 128), F32)],
        scratch_shapes=[pltpu.VMEM((rows, width), F32)],
        compiler_params=params(10),
        cost_estimate=cost(6 * rows * width * hidden, 8 * rows * hidden + 6 * width * hidden),
        name="backward_rows",
    )(*pieces, gate_factor, linear_factor, *out, *gate, *linear, *deps)
    return results[:3], results[3:-1], results[-1]


def weight_body(groups, kinds, column, add, deps, *refs):
    received = refs[5 * groups]
    out_refs = refs[5 * groups + (1 if add else 0) + deps :]
    mark_body(out_refs[-1])
    width, hidden = refs[0].shape[1], refs[2].shape[1]
    half, tile = width // 2, tile_of(hidden)
    side = slice(column * half, (column + 1) * half)

    @pl.loop(0, hidden // tile)
    def _(j):
        at = pl.ds(pl.multiple_of(j * tile, tile), tile)
        for place, kind in enumerate(kinds):
            total = None
            for g in range(groups):
                x_ref, b_ref, gate_delta, linear_delta, hid = refs[5 * g : 5 * g + 5]
                if kind == "out":
                    a, b = hid[:, at], b_ref[:, side]
                else:
                    a, b = x_ref[:, side], (gate_delta if kind == "gate" else linear_delta)[:, at]
                term = lax.dot_general(a, b, ROWS, preferred_element_type=F32)
                total = term if total is None else total + term
            rows = (at, slice(None)) if kind == "out" else (pl.ds(place * half, half), at)
            if add:
                total = total + received[rows].astype(F32)
                out_refs[place][at if kind == "out" else slice(None), slice(None) if kind == "out" else at] = (
                    total.astype(BF)
                )
            else:
                out_refs[0][rows] = total.astype(BF)


def weight_grads(groups, kinds, column, received, deps):
    hidden = groups[0][2].shape[1]
    half = groups[0][0].shape[1] // 2
    operands = [a for group in groups for a in group] + list(received)
    one = (hidden, half) if kinds == ("out",) else (half, hidden)
    shapes = [one] * len(kinds) if received else [(len(kinds) * one[0], one[1])]
    total_rows = sum(group[0].shape[0] for group in groups)
    return pl.pallas_call(
        functools.partial(
            weight_body, len(groups), kinds, column, bool(received), len(deps)
        ),
        in_specs=[VMEM] * len(operands) + [ANY] * len(deps),
        out_specs=[VMEM] * (len(shapes) + 1),
        out_shape=[jax.ShapeDtypeStruct(s, BF) for s in shapes]
        + [jax.ShapeDtypeStruct((8, 128), F32)],
        compiler_params=params(12),
        cost_estimate=cost(
            2 * len(kinds) * total_rows * half * hidden, 4 * total_rows * hidden
        ),
        name="weight_grads",
    )(*operands, *deps)


def finish_body(count, *refs):
    part_refs, (down_m, down_o), out_ref = refs[:count], refs[count : count + 2], refs[-1]
    total = part_refs[0][...].astype(F32)
    for ref in part_refs[1:]:
        total = total + ref[...].astype(F32)
    total = total.astype(BF)
    model, half = down_m.shape
    tile = tile_of(model)
    for start in range(0, model, tile):
        at = slice(start, start + tile)
        part = lax.dot_general(total[:, :half], down_m[at, :], LAST, preferred_element_type=F32)
        part += lax.dot_general(total[:, half:], down_o[at, :], LAST, preferred_element_type=F32)
        out_ref[:, at] = part.astype(BF)


def finish(parts, down, deps):
    tokens, model = parts[0].shape[0], down[0].shape[0]
    return pl.pallas_call(
        lambda *refs: finish_body(len(parts), *refs[: len(parts) + 2], refs[-1]),
        in_specs=[VMEM] * (len(parts) + 2) + [ANY] * len(deps),
        out_specs=VMEM,
        out_shape=jax.ShapeDtypeStruct((tokens, model), BF),
        compiler_params=params(10),
        cost_estimate=cost(2 * tokens * model * parts[0].shape[1], 4 * down[0].size),
        name="token_grad",
    )(*parts, *down, *deps)


def on_device(
    tokens,
    cotangent,
    expert_ids,
    slot_ids,
    gate_weights,
    latent_down,
    latent_up,
    expert_gate,
    expert_linear,
    expert_out,
):
    row_count = tokens.shape[0]
    pick_count = expert_ids.shape[1]
    group_count = lax.axis_size("expert")
    halves = lax.axis_size("half")
    expert_count = group_count * expert_gate.shape[0]
    capacity = min(
        row_count, 2 * ((9 * row_count * pick_count + 16 * expert_count - 1) // (16 * expert_count))
    )
    inner = group_count // PLANES
    fan = inner // SIDE

    def swap(a):
        return lax.ppermute(a, "dp", [(0, 1), (1, 0)])

    def along(a, shift):
        return lax.ppermute(
            a,
            "expert",
            [
                (z * inner + p, (z + shift) % PLANES * inner + p)
                for z in range(PLANES)
                for p in range(inner)
            ],
        )

    def beside(a):
        return lax.ppermute(a, "expert", [(i, i ^ 1) for i in range(group_count)])

    def across(parts):
        return [parts[0]] + [
            lax.ppermute(parts[k], "expert", [(i, i ^ (SIDE * k)) for i in range(group_count)])
            for k in range(1, fan)
        ]

    def summed(a):
        return lax.psum(a, "half") if halves > 1 else a

    last = []

    def deps(*extra):
        return [*last[-1:], *extra]

    def step(result):
        last.append(result[0] if isinstance(result, (list, tuple)) else result)
        return result

    def dot(a, weight, dims):
        if last:
            a = lax.optimization_barrier((a, last[-1]))[0]
        result = lax.dot_general(a, weight, dims, preferred_element_type=F32)
        return step(summed(result).astype(BF))

    def swapped_after(arrays, extra):
        held = lax.optimization_barrier((*arrays, *extra))[: len(arrays)]
        return [(a, swap(a)) for a in held]

    their_tokens, their_cotangent = swap(tokens), swap(cotangent)
    rows_first = (((1,), (0,)), ((), ()))
    latent_own = dot(tokens, latent_down, rows_first)
    latent_other = swap(dot(their_tokens, latent_down, rows_first))
    latent = step(
        join_rows(
            latent_own, latent_other, (expert_ids.T, slot_ids.T, gate_weights.T), deps()
        )
    )
    gate, linear, out = swapped_after(
        (expert_gate[0], expert_linear[0], expert_out[0]), (latent,)
    )
    back_own = dot(cotangent, latent_up, LAST)
    back_other = swap(dot(their_cotangent, latent_up, LAST))

    blocks, pairs, pieces = {("l", 0): latent}, {}, {}

    def to_plane(kind, c, *extra):
        block = blocks[kind, 0]
        if extra:
            block = step(tie(block, deps(*extra)))
        with jax.named_scope(f"plane_{kind}{c}"):
            blocks[kind, c] = along(block, c)

    def to_side(kind, c, tied=False):
        if tied:
            blocks[kind, c] = step(tie(blocks[kind, c], deps()))
        with jax.named_scope(f"side_{kind}{c}"):
            pairs[kind, c] = [blocks[kind, c], beside(blocks[kind, c])]

    def pick(kind, c, *extra):
        parts = step(
            select(
                pairs["l", c], pairs[kind, c], pick_count, fan, capacity, kind == "b", deps(*extra)
            )
        )
        with jax.named_scope(f"piece_{kind}{c}"):
            pieces[kind, c] = across(parts)

    def come(kind, c):
        return pieces[kind, c][-1]

    factors, saved, rows, partial = {}, {}, {}, {}

    def ahead(chunks):
        *factors[chunks], mark = forward(
            [a for c in chunks for a in pieces["l", c]], gate, linear, deps()
        )
        step(mark)

    def behind(chunks, *extra):
        x, gate_factor, linear_factor, hid = factors[chunks]
        (b, gate_delta, linear_delta), sums, mark = backward(
            [a for c in chunks for a in pieces["b", c]],
            gate_factor,
            linear_factor,
            out,
            gate,
            linear,
            deps(*extra),
        )
        step(mark)
        saved[chunks] = (x, b, gate_delta, linear_delta, hid)
        for i, c in enumerate(chunks):
            rows[c] = sums[i * fan : (i + 1) * fan]

    def send_rows(c, operands):
        with jax.named_scope(f"piece_r{c}"):
            rows[c] = across([rows[c][0], *operands])

    def send_side(c, results):
        own, other = results
        with jax.named_scope(f"side_r{c}"):
            partial[c] = [own, beside(other)]

    def send_home(c, results):
        with jax.named_scope(f"plane_r{c}"):
            partial[c] = along(results[0], -c)

    def turn(parts, through=(), extra=()):
        results, passed = bundle(parts, list(through), deps(*extra))
        step(results[0][0])
        return [*results, *passed]

    def gathered(c):
        return expanded(pairs["l", c], rows[c], pick_count, capacity, [F32, BF])

    to_plane("l", 1)
    to_side("l", 0)
    to_plane("l", 3, gate[1])
    back = step(join_rows(back_own, back_other, (), deps()))
    blocks["b", 0] = back
    pick("l", 0, blocks["l", 1], linear[1], out[1])
    to_side("l", 1)
    to_plane("l", 2, blocks["l", 1])
    pick("l", 1, blocks["l", 3])
    to_side("l", 3)
    to_plane("b", 2, blocks["l", 3])
    pick("l", 3, come("l", 0))
    to_side("b", 0)
    pick("b", 0, come("l", 1), blocks["l", 2])
    to_side("l", 2)
    to_plane("b", 3, blocks["l", 2])
    ahead((0, 1))
    pick("l", 2, come("l", 3), blocks["b", 2])
    to_side("b", 2)
    to_plane("b", 1, blocks["b", 2])
    (down,) = swapped_after((latent_down,), last[-1:])
    pick("b", 2, come("b", 0), blocks["b", 3])
    to_side("b", 3)
    pick("b", 3, come("l", 2), blocks["b", 1])
    to_side("b", 1)
    ahead((3, 2))
    pick("b", 1, come("b", 2), down[1])
    behind((3, 2))
    send_rows(3, rows[3][1:])
    behind((0, 1))
    results = turn([gathered(3), copies(rows[2][1:])])
    send_side(3, results[0])
    send_rows(2, results[1])
    groups = list(saved.values())

    def grads_of(kinds, column, *received):
        *results, mark = weight_grads(groups, kinds, column, received, deps())
        step(mark)
        return results

    wide = grads_of(("gate", "linear"), 1)
    results = turn([gathered(2), added(partial[3], BF), copies(rows[1][1:])], wide)
    send_side(2, results[0])
    send_home(3, results[1])
    send_rows(1, results[2])
    wide = swap(results[3])
    tall = grads_of(("out",), 1)
    results = turn([gathered(1), added(partial[2], BF), copies(rows[0][1:])], tall, [partial[3]])
    send_side(1, results[0])
    send_home(2, results[1])
    send_rows(0, results[2])
    tall = swap(results[3])
    grads = grads_of(("gate", "linear"), 0, wide)
    results = turn([gathered(0), added(partial[1], BF)], (), [])
    send_side(0, results[0])
    send_home(1, results[1])
    grads += grads_of(("out",), 0, tall)
    parts = [*partial[0], partial[1], partial[2], partial[3]]
    if halves > 1:
        results = turn([added(parts, F32)])
        parts = [summed(results[0][0])]
    token_grad = finish(parts, down, deps())
    return (token_grad, grads[0][None], grads[1][None], grads[2][None])


def solution(mesh):
    in_specs = (
        P(("expert", "dp"), "half"),
        P(("expert", "dp"), "half"),
        P(("expert", "dp"), None),
        P(("expert", "dp"), None),
        P(("expert", "dp"), None),
        P("half", "dp"),
        P("dp", "half"),
        P("expert", "dp", "half"),
        P("expert", "dp", "half"),
        P("expert", "half", "dp"),
    )
    out_specs = (
        P(("expert", "dp"), "half"),
        P("expert", "dp", "half"),
        P("expert", "dp", "half"),
        P("expert", "half", "dp"),
    )
    return jax.shard_map(
        on_device, mesh=mesh, in_specs=in_specs, out_specs=out_specs, check_vma=False
    )
```

```python
import functools

import jax
import jax.numpy as jnp
from jax import lax
from jax.experimental import pallas as pl
from jax.experimental.pallas import tpu as pltpu
from jax.sharding import PartitionSpec as P

BF = jnp.bfloat16
F32 = jnp.float32
PLANES = 4
SIDE = 2
META = 8
SIDE_TIE = True
SCALE = 1
MIB = 1024 * 1024
ROWS = (((0,), (0,)), ((), ()))
LAST = (((1,), (1,)), ((), ()))
ANY = pl.BlockSpec(memory_space=pl.ANY)
VMEM = pl.BlockSpec(memory_space=pltpu.VMEM)


def pad16(n):
    return (n + 15) // 16 * 16


def params(mib):
    return pltpu.CompilerParams(vmem_limit_bytes=mib * MIB)


def cost(flops, moved):
    return pl.CostEstimate(flops=int(flops * SCALE) + 1, bytes_accessed=int(moved * SCALE) + 1, transcendentals=0)


def whole(shape):
    return pl.BlockSpec(shape, lambda *_: (0,) * len(shape))


def join_body(routes, own_ref, other_ref, *refs):
    out_ref = refs[-1]
    tokens, half = own_ref.shape
    out_ref[:tokens, :half] = own_ref[...]
    out_ref[:tokens, half:] = other_ref[...]
    if routes:
        ids_ref, slots_ref, gates_ref = refs[:3]
        gates = gates_ref[...]
        high = gates.astype(BF)
        rest = gates - high.astype(F32)
        middle = rest.astype(BF)
        low = (rest - middle.astype(F32)).astype(BF)
        kinds = [ids_ref[...].astype(F32).astype(BF), slots_ref[...].astype(F32).astype(BF)]
        kinds += [high, middle, low]
        kinds += [jnp.zeros_like(low)] * (META - len(kinds))
        picks = gates.shape[0]
        table = jnp.concatenate([a.astype(F32) for a in kinds], axis=1)
        table = jnp.concatenate(
            [table, jnp.zeros((pad16(picks) - picks, table.shape[1]), F32)], axis=0
        )
        out_ref[tokens:, :] = table.astype(BF)


def join_rows(own, other, routes, deps):
    tokens, half = own.shape
    extra = pad16(routes[0].shape[0]) if routes else 0
    return pl.pallas_call(
        functools.partial(join_body, bool(routes)),
        out_shape=jax.ShapeDtypeStruct((tokens + extra, 2 * half), BF),
        in_specs=[VMEM] * (2 + len(routes)) + [ANY] * len(deps),
        out_specs=VMEM,
        compiler_params=params(8),
        cost_estimate=cost(0, 8 * tokens * half),
        name="join_rows",
    )(own, other, *routes, *deps)


def tie_body(block_ref, *refs):
    refs[-1][...] = block_ref[...]


def tie(block, deps):
    return pl.pallas_call(
        tie_body,
        out_shape=jax.ShapeDtypeStruct(block.shape, block.dtype),
        in_specs=[VMEM] + [ANY] * len(deps),
        out_specs=VMEM,
        compiler_params=params(8),
        cost_estimate=cost(0, 4 * block.size),
        name="tie_rows",
    )(block, *deps)


def one_hots(meta_refs, picks, fan, cap, weighted):
    me = lax.axis_index("expert")
    padded = pad16(len(meta_refs) * cap)
    marks, total = [], None
    for j, ref in enumerate(meta_refs):
        tokens = ref.shape[1] // META
        start = ref.shape[0] - pad16(picks)
        kinds = [
            ref[start:, i * tokens : (i + 1) * tokens].astype(F32)
            for i in range(5 if weighted else 2)
        ]
        held = kinds[0] * cap + kinds[1]
        row = lax.broadcasted_iota(jnp.int32, (padded, tokens), 0)
        inside = jnp.logical_and(row >= j * cap, row < (j + 1) * cap)
        targets = []
        for k in range(fan):
            base = lax.bitwise_xor(me, SIDE * k) * cap - j * cap
            targets.append(jnp.where(inside, row + base, -1))
        target = jnp.concatenate(targets, axis=0).astype(F32)
        mark = jnp.zeros(target.shape, F32)
        weight = jnp.zeros(target.shape, F32)
        if weighted:
            gate = kinds[2] + kinds[3] + kinds[4]
        for i in range(picks):
            equal = target == held[i : i + 1, :]
            mark = jnp.where(equal, 1.0, mark)
            if weighted:
                weight = jnp.where(equal, gate[i : i + 1, :], weight)
        marks.append(mark.astype(BF))
        if weighted:
            weight = jnp.sum(weight, axis=1, keepdims=True)
            total = weight if total is None else total + weight
    return marks, total


def select_body(count, picks, fan, cap, weighted, deps, *refs):
    meta_refs, block_refs, piece_refs = refs[:count], refs[count : 2 * count], refs[2 * count + deps :]
    marks, weight = one_hots(meta_refs, picks, fan, cap, weighted)
    tokens = marks[0].shape[1]
    rows = None
    for mark, block_ref in zip(marks, block_refs):
        term = jnp.dot(mark, block_ref[:tokens, :], preferred_element_type=F32)
        rows = term if rows is None else rows + term
    if weighted:
        rows = rows * weight
    padded = pad16(count * cap)
    for k in range(fan):
        piece_refs[k][...] = rows[k * padded : k * padded + count * cap, :].astype(BF)


def select(metas, blocks, picks, fan, cap, weighted, deps):
    count = len(blocks)
    width = blocks[0].shape[1]
    tokens = width // META
    return pl.pallas_call(
        functools.partial(select_body, count, picks, fan, cap, weighted, len(deps)),
        out_shape=[jax.ShapeDtypeStruct((count * cap, width), BF)] * fan,
        in_specs=[VMEM] * (2 * count) + [ANY] * len(deps),
        out_specs=[VMEM] * fan,
        compiler_params=params(10),
        cost_estimate=cost(
            2 * fan * count * count * cap * tokens * width, 8 * count * tokens * width
        ),
        name="select_back" if weighted else "select_latent",
    )(*metas, *blocks, *deps)


def assemble(piece_refs, out_ref):
    rows = piece_refs[0].shape[0]
    padded = pad16(rows)
    for i, ref in enumerate(piece_refs):
        if padded > rows:
            out_ref[(i + 1) * padded - 16 : (i + 1) * padded, :] = jnp.zeros(
                (16, out_ref.shape[1]), out_ref.dtype
            )
        out_ref[i * padded : i * padded + rows, :] = ref[...]


def bundle_body(parts, held_over, deps, *refs):
    at = sum(len(part[1]) for part in parts)
    ins, refs = refs[:at], refs[at + held_over + deps :]
    outs_count = sum(len(part[2]) for part in parts)
    outs, scratch = refs[:outs_count], refs[outs_count + held_over :]
    for body, operands, results, held in parts:
        body(*ins[: len(operands)], *outs[: len(results)], *scratch[: len(held)])
        ins, outs, scratch = ins[len(operands) :], outs[len(results) :], scratch[len(held) :]


def bundle(parts, through, deps):
    operands = [a for part in parts for a in part[1]]
    shapes = [a for part in parts for a in part[2]]
    sizes = sum(a.size for a in operands)
    results = pl.pallas_call(
        functools.partial(bundle_body, parts, len(through), len(deps)),
        out_shape=shapes + [jax.ShapeDtypeStruct(a.shape, a.dtype) for a in through],
        in_specs=[VMEM] * len(operands) + [ANY] * (len(through) + len(deps)),
        out_specs=[VMEM] * len(shapes) + [ANY] * len(through),
        input_output_aliases={len(operands) + i: len(shapes) + i for i in range(len(through))},
        scratch_shapes=[a for part in parts for a in part[3]],
        compiler_params=params(10),
        cost_estimate=cost(0, 4 * sizes),
        name="return_rows",
    )(*operands, *through, *deps)
    split = []
    for part in parts:
        split.append(results[: len(part[2])])
        results = results[len(part[2]) :]
    return split, results


def copy_body(count, *refs):
    for i in range(count):
        refs[count + i][...] = refs[i][...]


def copies(arrays):
    shapes = [jax.ShapeDtypeStruct(a.shape, a.dtype) for a in arrays]
    return functools.partial(copy_body, len(arrays)), list(arrays), shapes, []


def mark_body(mark_ref):
    mark_ref[...] = jnp.zeros_like(mark_ref)


MARK = (mark_body, [], [jax.ShapeDtypeStruct((8, 128), F32)], [])


def add_body(count, *refs):
    total = refs[0][...].astype(F32)
    for ref in refs[1:count]:
        total = total + ref[...].astype(F32)
    refs[count][...] = total.astype(refs[count].dtype)


def added(arrays, dtype):
    shape = jax.ShapeDtypeStruct(arrays[0].shape, dtype)
    return functools.partial(add_body, len(arrays)), list(arrays), [shape], []


def expand_body(count, picks, fan, cap, *refs):
    meta_refs, piece_refs = refs[:count], refs[count : count + fan]
    out_refs, held = refs[count + fan : -1], refs[-1]
    assemble(piece_refs, held)
    marks, _ = one_hots(meta_refs, picks, fan, cap, False)
    for mark, out_ref in zip(marks, out_refs):
        out_ref[...] = lax.dot_general(
            mark, held[...], ROWS, preferred_element_type=F32
        ).astype(out_ref.dtype)


def expanded(metas, pieces, picks, cap, dtypes):
    count, fan = len(metas), len(pieces)
    width = pieces[0].shape[1]
    return (
        functools.partial(expand_body, count, picks, fan, cap),
        [*metas, *pieces],
        [jax.ShapeDtypeStruct((width // META, width), d) for d in dtypes],
        [pltpu.VMEM((fan * pad16(count * cap), width), BF)],
    )


def tile_of(hidden):
    return 512 if hidden % 512 == 0 else 256


def forward_body(count, deps, *refs):
    piece_refs = refs[:count]
    gate_m, gate_o, linear_m, linear_o = refs[count : count + 4]
    x_ref, gate_factor_ref, linear_factor_ref, hidden_ref, mark_ref = refs[count + 4 + deps :]
    mark_body(mark_ref)
    assemble(piece_refs, x_ref)
    half, hidden = gate_m.shape
    tile = tile_of(hidden)
    @pl.loop(0, hidden // tile)
    def _(j):
        at = pl.ds(pl.multiple_of(j * tile, tile), tile)
        pre_gate = jnp.dot(x_ref[:, :half], gate_m[:, at], preferred_element_type=F32)
        pre_gate += jnp.dot(x_ref[:, half:], gate_o[:, at], preferred_element_type=F32)
        pre_linear = jnp.dot(x_ref[:, :half], linear_m[:, at], preferred_element_type=F32)
        pre_linear += jnp.dot(x_ref[:, half:], linear_o[:, at], preferred_element_type=F32)
        logistic = jax.nn.sigmoid(pre_gate)
        scaled = pre_gate * logistic
        hidden_ref[:, at] = (scaled * pre_linear).astype(BF)
        linear_factor_ref[:, at] = scaled.astype(BF)
        gate_factor_ref[:, at] = (
            pre_linear * logistic * (1.0 + pre_gate * (1.0 - logistic))
        ).astype(BF)


def forward(pieces, gate, linear, deps):
    count = len(pieces)
    size, width = pieces[0].shape
    rows = count * pad16(size)
    hidden = gate[0].shape[1]
    return pl.pallas_call(
        functools.partial(forward_body, count, len(deps)),
        in_specs=[VMEM] * (count + 4) + [ANY] * len(deps),
        out_specs=[VMEM] * 5,
        out_shape=[jax.ShapeDtypeStruct((rows, width), BF)]
        + [jax.ShapeDtypeStruct((rows, hidden), BF)] * 3
        + [jax.ShapeDtypeStruct((8, 128), F32)],
        compiler_params=params(10),
        cost_estimate=cost(4 * rows * width * hidden, 6 * rows * hidden + 4 * width * hidden),
        name="forward_rows",
    )(*pieces, *gate, *linear, *deps)


def backward_body(count, deps, *refs):
    piece_refs = refs[:count]
    gate_factor, linear_factor, out_m, out_o = refs[count : count + 4]
    gate_m, gate_o, linear_m, linear_o = refs[count + 4 : count + 8]
    refs = refs[count + 8 + deps :]
    b_ref, gate_delta_ref, linear_delta_ref = refs[:3]
    row_refs, mark_ref, total = refs[3:-2], refs[-2], refs[-1]
    mark_body(mark_ref)
    assemble(piece_refs, b_ref)
    hidden, half = out_m.shape
    tile = tile_of(hidden)
    for start in range(0, hidden, tile):
        at = slice(start, start + tile)
        grad = lax.dot_general(b_ref[:, :half], out_m[at, :], LAST, preferred_element_type=F32)
        grad += lax.dot_general(b_ref[:, half:], out_o[at, :], LAST, preferred_element_type=F32)
        gate_delta_ref[:, at] = (grad * gate_factor[:, at].astype(F32)).astype(BF)
        linear_delta_ref[:, at] = (grad * linear_factor[:, at].astype(F32)).astype(BF)
    for start, gate, linear in ((0, gate_m, linear_m), (half, gate_o, linear_o)):
        part = lax.dot_general(gate_delta_ref[...], gate[...], LAST, preferred_element_type=F32)
        part += lax.dot_general(
            linear_delta_ref[...], linear[...], LAST, preferred_element_type=F32
        )
        total[:, start : start + half] = part
    size = row_refs[0].shape[0]
    for i, ref in enumerate(row_refs):
        start = i * pad16(size)
        ref[...] = total[start : start + size, :].astype(BF)


def backward(pieces, gate_factor, linear_factor, out, gate, linear, deps):
    count = len(pieces)
    size, width = pieces[0].shape
    rows = count * pad16(size)
    hidden = gate_factor.shape[1]
    results = pl.pallas_call(
        functools.partial(backward_body, count, len(deps)),
        in_specs=[VMEM] * (count + 8) + [ANY] * len(deps),
        out_specs=[VMEM] * (4 + count),
        out_shape=[jax.ShapeDtypeStruct((rows, width), BF)]
        + [jax.ShapeDtypeStruct((rows, hidden), BF)] * 2
        + [jax.ShapeDtypeStruct((size, width), BF)] * count
        + [jax.ShapeDtypeStruct((8, 128), F32)],
        scratch_shapes=[pltpu.VMEM((rows, width), F32)],
        compiler_params=params(10),
        cost_estimate=cost(6 * rows * width * hidden, 8 * rows * hidden + 6 * width * hidden),
        name="backward_rows",
    )(*pieces, gate_factor, linear_factor, *out, *gate, *linear, *deps)
    return results[:3], results[3:-1], results[-1]


def weight_body(groups, kinds, column, add, deps, *refs):
    received = refs[5 * groups]
    out_refs = refs[5 * groups + (1 if add else 0) + deps :]
    mark_body(out_refs[-1])
    width, hidden = refs[0].shape[1], refs[2].shape[1]
    half, tile = width // 2, tile_of(hidden)
    side = slice(column * half, (column + 1) * half)

    @pl.loop(0, hidden // tile)
    def _(j):
        at = pl.ds(pl.multiple_of(j * tile, tile), tile)
        for place, kind in enumerate(kinds):
            total = None
            for g in range(groups):
                x_ref, b_ref, gate_delta, linear_delta, hid = refs[5 * g : 5 * g + 5]
                if kind == "out":
                    a, b = hid[:, at], b_ref[:, side]
                else:
                    a, b = x_ref[:, side], (gate_delta if kind == "gate" else linear_delta)[:, at]
                term = lax.dot_general(a, b, ROWS, preferred_element_type=F32)
                total = term if total is None else total + term
            rows = (at, slice(None)) if kind == "out" else (pl.ds(place * half, half), at)
            if add:
                total = total + received[rows].astype(F32)
                out_refs[place][at if kind == "out" else slice(None), slice(None) if kind == "out" else at] = (
                    total.astype(BF)
                )
            else:
                out_refs[0][rows] = total.astype(BF)


def weight_grads(groups, kinds, column, received, deps):
    hidden = groups[0][2].shape[1]
    half = groups[0][0].shape[1] // 2
    operands = [a for group in groups for a in group] + list(received)
    one = (hidden, half) if kinds == ("out",) else (half, hidden)
    shapes = [one] * len(kinds) if received else [(len(kinds) * one[0], one[1])]
    total_rows = sum(group[0].shape[0] for group in groups)
    return pl.pallas_call(
        functools.partial(
            weight_body, len(groups), kinds, column, bool(received), len(deps)
        ),
        in_specs=[VMEM] * len(operands) + [ANY] * len(deps),
        out_specs=[VMEM] * (len(shapes) + 1),
        out_shape=[jax.ShapeDtypeStruct(s, BF) for s in shapes]
        + [jax.ShapeDtypeStruct((8, 128), F32)],
        compiler_params=params(12),
        cost_estimate=cost(
            2 * len(kinds) * total_rows * half * hidden, 4 * total_rows * hidden
        ),
        name="weight_grads",
    )(*operands, *deps)


def finish_body(count, *refs):
    part_refs, (down_m, down_o), out_ref = refs[:count], refs[count : count + 2], refs[-1]
    total = part_refs[0][...].astype(F32)
    for ref in part_refs[1:]:
        total = total + ref[...].astype(F32)
    total = total.astype(BF)
    model, half = down_m.shape
    tile = tile_of(model)
    for start in range(0, model, tile):
        at = slice(start, start + tile)
        part = lax.dot_general(total[:, :half], down_m[at, :], LAST, preferred_element_type=F32)
        part += lax.dot_general(total[:, half:], down_o[at, :], LAST, preferred_element_type=F32)
        out_ref[:, at] = part.astype(BF)


def finish(parts, down, deps):
    tokens, model = parts[0].shape[0], down[0].shape[0]
    return pl.pallas_call(
        lambda *refs: finish_body(len(parts), *refs[: len(parts) + 2], refs[-1]),
        in_specs=[VMEM] * (len(parts) + 2) + [ANY] * len(deps),
        out_specs=VMEM,
        out_shape=jax.ShapeDtypeStruct((tokens, model), BF),
        compiler_params=params(10),
        cost_estimate=cost(2 * tokens * model * parts[0].shape[1], 4 * down[0].size),
        name="token_grad",
    )(*parts, *down, *deps)


def on_device(
    tokens,
    cotangent,
    expert_ids,
    slot_ids,
    gate_weights,
    latent_down,
    latent_up,
    expert_gate,
    expert_linear,
    expert_out,
):
    row_count = tokens.shape[0]
    pick_count = expert_ids.shape[1]
    group_count = lax.axis_size("expert")
    halves = lax.axis_size("half")
    expert_count = group_count * expert_gate.shape[0]
    capacity = min(
        row_count, 2 * ((9 * row_count * pick_count + 16 * expert_count - 1) // (16 * expert_count))
    )
    inner = group_count // PLANES
    fan = inner // SIDE

    def swap(a):
        return lax.ppermute(a, "dp", [(0, 1), (1, 0)])

    def along(a, shift):
        return lax.ppermute(
            a,
            "expert",
            [
                (z * inner + p, (z + shift) % PLANES * inner + p)
                for z in range(PLANES)
                for p in range(inner)
            ],
        )

    def beside(a):
        return lax.ppermute(a, "expert", [(i, i ^ 1) for i in range(group_count)])

    def across(parts):
        return [parts[0]] + [
            lax.ppermute(parts[k], "expert", [(i, i ^ (SIDE * k)) for i in range(group_count)])
            for k in range(1, fan)
        ]

    def summed(a):
        return lax.psum(a, "half") if halves > 1 else a

    last = []

    def deps(*extra):
        return [*last[-1:], *extra]

    def step(result):
        last.append(result[0] if isinstance(result, (list, tuple)) else result)
        return result

    def dot(a, weight, dims):
        if last:
            a = lax.optimization_barrier((a, last[-1]))[0]
        result = lax.dot_general(a, weight, dims, preferred_element_type=F32)
        return step(summed(result).astype(BF))

    def swapped_after(arrays, extra):
        held = lax.optimization_barrier((*arrays, *extra))[: len(arrays)]
        return [(a, swap(a)) for a in held]

    their_tokens, their_cotangent = swap(tokens), swap(cotangent)
    rows_first = (((1,), (0,)), ((), ()))
    latent_own = dot(tokens, latent_down, rows_first)
    latent_other = swap(dot(their_tokens, latent_down, rows_first))
    latent = step(
        join_rows(
            latent_own, latent_other, (expert_ids.T, slot_ids.T, gate_weights.T), deps()
        )
    )
    gate, linear, out = swapped_after(
        (expert_gate[0], expert_linear[0], expert_out[0]), (latent,)
    )
    back_own = dot(cotangent, latent_up, LAST)
    back_other = swap(dot(their_cotangent, latent_up, LAST))

    blocks, pairs, pieces = {("l", 0): latent}, {}, {}

    def to_plane(kind, c, *extra):
        block = blocks[kind, 0]
        if extra:
            block = step(tie(block, deps(*extra)))
        with jax.named_scope(f"plane_{kind}{c}"):
            blocks[kind, c] = along(block, c)

    def to_side(kind, c, tied=False):
        if tied:
            blocks[kind, c] = step(tie(blocks[kind, c], deps()))
        with jax.named_scope(f"side_{kind}{c}"):
            pairs[kind, c] = [blocks[kind, c], beside(blocks[kind, c])]

    def pick(kind, c, *extra):
        parts = step(
            select(
                pairs["l", c], pairs[kind, c], pick_count, fan, capacity, kind == "b", deps(*extra)
            )
        )
        with jax.named_scope(f"piece_{kind}{c}"):
            pieces[kind, c] = across(parts)

    def come(kind, c):
        return pieces[kind, c][-1]

    factors, saved, rows, partial = {}, {}, {}, {}

    def ahead(chunks):
        *factors[chunks], mark = forward(
            [a for c in chunks for a in pieces["l", c]], gate, linear, deps()
        )
        step(mark)

    def behind(chunks, *extra):
        x, gate_factor, linear_factor, hid = factors[chunks]
        (b, gate_delta, linear_delta), sums, mark = backward(
            [a for c in chunks for a in pieces["b", c]],
            gate_factor,
            linear_factor,
            out,
            gate,
            linear,
            deps(*extra),
        )
        step(mark)
        saved[chunks] = (x, b, gate_delta, linear_delta, hid)
        for i, c in enumerate(chunks):
            rows[c] = sums[i * fan : (i + 1) * fan]

    def send_rows(c, operands):
        with jax.named_scope(f"piece_r{c}"):
            rows[c] = across([rows[c][0], *operands])

    def send_side(c, results):
        own, other = results
        with jax.named_scope(f"side_r{c}"):
            partial[c] = [own, beside(other)]

    def send_home(c, results):
        with jax.named_scope(f"plane_r{c}"):
            partial[c] = along(results[0], -c)

    def turn(parts, through=(), extra=()):
        results, passed = bundle(parts, list(through), deps(*extra))
        step(results[0][0])
        return [*results, *passed]

    def gathered(c):
        return expanded(pairs["l", c], rows[c], pick_count, capacity, [F32, BF])

    to_plane("l", 1)
    to_side("l", 0)
    to_plane("l", 3, gate[1])
    back = step(join_rows(back_own, back_other, (), deps()))
    blocks["b", 0] = back
    pick("l", 0, blocks["l", 1], linear[1], out[1])
    to_side("l", 1)
    to_plane("l", 2, blocks["l", 1])
    pick("l", 1, blocks["l", 3])
    to_side("l", 3)
    to_plane("b", 2, blocks["l", 3])
    pick("l", 3, come("l", 0))
    to_side("b", 0)
    pick("b", 0, come("l", 1), blocks["l", 2])
    to_side("l", 2)
    to_plane("b", 3, blocks["l", 2])
    ahead((0, 1))
    pick("l", 2, come("l", 3), blocks["b", 2])
    to_side("b", 2)
    to_plane("b", 1, blocks["b", 2])
    (down,) = swapped_after((latent_down,), last[-1:])
    pick("b", 2, come("b", 0), blocks["b", 3])
    to_side("b", 3)
    pick("b", 3, come("l", 2), blocks["b", 1])
    to_side("b", 1)
    ahead((3, 2))
    pick("b", 1, come("b", 2))
    behind((3, 2))
    send_rows(3, rows[3][1:])
    behind((0, 1))
    results = turn([gathered(3), copies(rows[2][1:])])
    send_side(3, results[0])
    send_rows(2, results[1])
    groups = list(saved.values())

    def grads_of(kinds, column, *received):
        *results, mark = weight_grads(groups, kinds, column, received, deps())
        step(mark)
        return results

    wide = grads_of(("gate", "linear"), 1)
    results = turn([gathered(2), added(partial[3], BF), copies(rows[1][1:])], wide)
    send_side(2, results[0])
    send_home(3, results[1])
    send_rows(1, results[2])
    wide = swap(results[3])
    tall = grads_of(("out",), 1)
    results = turn([gathered(1), added(partial[2], BF), copies(rows[0][1:])], tall, [partial[3]])
    send_side(1, results[0])
    send_home(2, results[1])
    send_rows(0, results[2])
    tall = swap(results[3])
    grads = grads_of(("gate", "linear"), 0, wide)
    results = turn([gathered(0), added(partial[1], BF)], (), [])
    send_side(0, results[0])
    send_home(1, results[1])
    grads += grads_of(("out",), 0, tall)
    parts = [*partial[0], partial[1], partial[2], partial[3]]
    if halves > 1:
        results = turn([added(parts, F32)])
        parts = [summed(results[0][0])]
    token_grad = finish(parts, down, deps())
    return (token_grad, grads[0][None], grads[1][None], grads[2][None])


def solution(mesh):
    in_specs = (
        P(("expert", "dp"), "half"),
        P(("expert", "dp"), "half"),
        P(("expert", "dp"), None),
        P(("expert", "dp"), None),
        P(("expert", "dp"), None),
        P("half", "dp"),
        P("dp", "half"),
        P("expert", "dp", "half"),
        P("expert", "dp", "half"),
        P("expert", "half", "dp"),
    )
    out_specs = (
        P(("expert", "dp"), "half"),
        P("expert", "dp", "half"),
        P("expert", "dp", "half"),
        P("expert", "half", "dp"),
    )
    return jax.shard_map(
        on_device, mesh=mesh, in_specs=in_specs, out_specs=out_specs, check_vma=False
    )
```

```python
import functools

import jax
import jax.numpy as jnp
from jax import lax
from jax.experimental import pallas as pl
from jax.experimental.pallas import tpu as pltpu
from jax.sharding import PartitionSpec as P

BF = jnp.bfloat16
F32 = jnp.float32
PLANES = 4
SIDE = 2
META = 8
SIDE_TIE = True
SCALE = 1
MIB = 1024 * 1024
ROWS = (((0,), (0,)), ((), ()))
LAST = (((1,), (1,)), ((), ()))
ANY = pl.BlockSpec(memory_space=pl.ANY)
VMEM = pl.BlockSpec(memory_space=pltpu.VMEM)


def pad16(n):
    return (n + 15) // 16 * 16


def params(mib):
    return pltpu.CompilerParams(vmem_limit_bytes=mib * MIB)


def cost(flops, moved):
    return pl.CostEstimate(flops=int(flops * SCALE) + 1, bytes_accessed=int(moved * SCALE) + 1, transcendentals=0)


def whole(shape):
    return pl.BlockSpec(shape, lambda *_: (0,) * len(shape))


def join_body(routes, own_ref, other_ref, *refs):
    out_ref = refs[-1]
    tokens, half = own_ref.shape
    out_ref[:tokens, :half] = own_ref[...]
    out_ref[:tokens, half:] = other_ref[...]
    if routes:
        ids_ref, slots_ref, gates_ref = refs[:3]
        gates = gates_ref[...]
        high = gates.astype(BF)
        rest = gates - high.astype(F32)
        middle = rest.astype(BF)
        low = (rest - middle.astype(F32)).astype(BF)
        kinds = [ids_ref[...].astype(F32).astype(BF), slots_ref[...].astype(F32).astype(BF)]
        kinds += [high, middle, low]
        kinds += [jnp.zeros_like(low)] * (META - len(kinds))
        picks = gates.shape[0]
        table = jnp.concatenate([a.astype(F32) for a in kinds], axis=1)
        table = jnp.concatenate(
            [table, jnp.zeros((pad16(picks) - picks, table.shape[1]), F32)], axis=0
        )
        out_ref[tokens:, :] = table.astype(BF)


def join_rows(own, other, routes, deps):
    tokens, half = own.shape
    extra = pad16(routes[0].shape[0]) if routes else 0
    return pl.pallas_call(
        functools.partial(join_body, bool(routes)),
        out_shape=jax.ShapeDtypeStruct((tokens + extra, 2 * half), BF),
        in_specs=[VMEM] * (2 + len(routes)) + [ANY] * len(deps),
        out_specs=VMEM,
        compiler_params=params(8),
        cost_estimate=cost(0, 8 * tokens * half),
        name="join_rows",
    )(own, other, *routes, *deps)


def tie_body(block_ref, *refs):
    refs[-1][...] = block_ref[...]


def tie(block, deps):
    return pl.pallas_call(
        tie_body,
        out_shape=jax.ShapeDtypeStruct(block.shape, block.dtype),
        in_specs=[VMEM] + [ANY] * len(deps),
        out_specs=VMEM,
        compiler_params=params(8),
        cost_estimate=cost(0, 4 * block.size),
        name="tie_rows",
    )(block, *deps)


def one_hots(meta_refs, picks, fan, cap, weighted):
    me = lax.axis_index("expert")
    padded = pad16(len(meta_refs) * cap)
    marks, total = [], None
    for j, ref in enumerate(meta_refs):
        tokens = ref.shape[1] // META
        start = ref.shape[0] - pad16(picks)
        kinds = [
            ref[start:, i * tokens : (i + 1) * tokens].astype(F32)
            for i in range(5 if weighted else 2)
        ]
        held = kinds[0] * cap + kinds[1]
        row = lax.broadcasted_iota(jnp.int32, (padded, tokens), 0)
        inside = jnp.logical_and(row >= j * cap, row < (j + 1) * cap)
        targets = []
        for k in range(fan):
            base = lax.bitwise_xor(me, SIDE * k) * cap - j * cap
            targets.append(jnp.where(inside, row + base, -1))
        target = jnp.concatenate(targets, axis=0).astype(F32)
        mark = jnp.zeros(target.shape, F32)
        weight = jnp.zeros(target.shape, F32)
        if weighted:
            gate = kinds[2] + kinds[3] + kinds[4]
        for i in range(picks):
            equal = target == held[i : i + 1, :]
            mark = jnp.where(equal, 1.0, mark)
            if weighted:
                weight = jnp.where(equal, gate[i : i + 1, :], weight)
        marks.append(mark.astype(BF))
        if weighted:
            weight = jnp.sum(weight, axis=1, keepdims=True)
            total = weight if total is None else total + weight
    return marks, total


def select_body(count, picks, fan, cap, weighted, deps, *refs):
    meta_refs, block_refs, piece_refs = refs[:count], refs[count : 2 * count], refs[2 * count + deps :]
    marks, weight = one_hots(meta_refs, picks, fan, cap, weighted)
    tokens = marks[0].shape[1]
    rows = None
    for mark, block_ref in zip(marks, block_refs):
        term = jnp.dot(mark, block_ref[:tokens, :], preferred_element_type=F32)
        rows = term if rows is None else rows + term
    if weighted:
        rows = rows * weight
    padded = pad16(count * cap)
    for k in range(fan):
        piece_refs[k][...] = rows[k * padded : k * padded + count * cap, :].astype(BF)


def select(metas, blocks, picks, fan, cap, weighted, deps):
    count = len(blocks)
    width = blocks[0].shape[1]
    tokens = width // META
    return pl.pallas_call(
        functools.partial(select_body, count, picks, fan, cap, weighted, len(deps)),
        out_shape=[jax.ShapeDtypeStruct((count * cap, width), BF)] * fan,
        in_specs=[VMEM] * (2 * count) + [ANY] * len(deps),
        out_specs=[VMEM] * fan,
        compiler_params=params(10),
        cost_estimate=cost(
            2 * fan * count * count * cap * tokens * width, 8 * count * tokens * width
        ),
        name="select_back" if weighted else "select_latent",
    )(*metas, *blocks, *deps)


def assemble(piece_refs, out_ref):
    rows = piece_refs[0].shape[0]
    padded = pad16(rows)
    for i, ref in enumerate(piece_refs):
        if padded > rows:
            out_ref[(i + 1) * padded - 16 : (i + 1) * padded, :] = jnp.zeros(
                (16, out_ref.shape[1]), out_ref.dtype
            )
        out_ref[i * padded : i * padded + rows, :] = ref[...]


def bundle_body(parts, held_over, deps, *refs):
    at = sum(len(part[1]) for part in parts)
    ins, refs = refs[:at], refs[at + held_over + deps :]
    outs_count = sum(len(part[2]) for part in parts)
    outs, scratch = refs[:outs_count], refs[outs_count + held_over :]
    for body, operands, results, held in parts:
        body(*ins[: len(operands)], *outs[: len(results)], *scratch[: len(held)])
        ins, outs, scratch = ins[len(operands) :], outs[len(results) :], scratch[len(held) :]


def bundle(parts, through, deps):
    operands = [a for part in parts for a in part[1]]
    shapes = [a for part in parts for a in part[2]]
    sizes = sum(a.size for a in operands)
    results = pl.pallas_call(
        functools.partial(bundle_body, parts, len(through), len(deps)),
        out_shape=shapes + [jax.ShapeDtypeStruct(a.shape, a.dtype) for a in through],
        in_specs=[VMEM] * len(operands) + [ANY] * (len(through) + len(deps)),
        out_specs=[VMEM] * len(shapes) + [ANY] * len(through),
        input_output_aliases={len(operands) + i: len(shapes) + i for i in range(len(through))},
        scratch_shapes=[a for part in parts for a in part[3]],
        compiler_params=params(10),
        cost_estimate=cost(0, 4 * sizes),
        name="return_rows",
    )(*operands, *through, *deps)
    split = []
    for part in parts:
        split.append(results[: len(part[2])])
        results = results[len(part[2]) :]
    return split, results


def copy_body(count, *refs):
    for i in range(count):
        refs[count + i][...] = refs[i][...]


def copies(arrays):
    shapes = [jax.ShapeDtypeStruct(a.shape, a.dtype) for a in arrays]
    return functools.partial(copy_body, len(arrays)), list(arrays), shapes, []


def mark_body(mark_ref):
    mark_ref[...] = jnp.zeros_like(mark_ref)


MARK = (mark_body, [], [jax.ShapeDtypeStruct((8, 128), F32)], [])


def add_body(count, *refs):
    total = refs[0][...].astype(F32)
    for ref in refs[1:count]:
        total = total + ref[...].astype(F32)
    refs[count][...] = total.astype(refs[count].dtype)


def added(arrays, dtype):
    shape = jax.ShapeDtypeStruct(arrays[0].shape, dtype)
    return functools.partial(add_body, len(arrays)), list(arrays), [shape], []


def expand_body(count, picks, fan, cap, *refs):
    meta_refs, piece_refs = refs[:count], refs[count : count + fan]
    out_refs, held = refs[count + fan : -1], refs[-1]
    assemble(piece_refs, held)
    marks, _ = one_hots(meta_refs, picks, fan, cap, False)
    for mark, out_ref in zip(marks, out_refs):
        out_ref[...] = lax.dot_general(
            mark, held[...], ROWS, preferred_element_type=F32
        ).astype(out_ref.dtype)


def expanded(metas, pieces, picks, cap, dtypes):
    count, fan = len(metas), len(pieces)
    width = pieces[0].shape[1]
    return (
        functools.partial(expand_body, count, picks, fan, cap),
        [*metas, *pieces],
        [jax.ShapeDtypeStruct((width // META, width), d) for d in dtypes],
        [pltpu.VMEM((fan * pad16(count * cap), width), BF)],
    )


def tile_of(hidden):
    return 512 if hidden % 512 == 0 else 256


def forward_body(count, deps, *refs):
    piece_refs = refs[:count]
    gate_m, gate_o, linear_m, linear_o = refs[count : count + 4]
    x_ref, gate_factor_ref, linear_factor_ref, hidden_ref, mark_ref = refs[count + 4 + deps :]
    mark_body(mark_ref)
    assemble(piece_refs, x_ref)
    half, hidden = gate_m.shape
    tile = tile_of(hidden)
    @pl.loop(0, hidden // tile)
    def _(j):
        at = pl.ds(pl.multiple_of(j * tile, tile), tile)
        pre_gate = jnp.dot(x_ref[:, :half], gate_m[:, at], preferred_element_type=F32)
        pre_gate += jnp.dot(x_ref[:, half:], gate_o[:, at], preferred_element_type=F32)
        pre_linear = jnp.dot(x_ref[:, :half], linear_m[:, at], preferred_element_type=F32)
        pre_linear += jnp.dot(x_ref[:, half:], linear_o[:, at], preferred_element_type=F32)
        logistic = jax.nn.sigmoid(pre_gate)
        scaled = pre_gate * logistic
        hidden_ref[:, at] = (scaled * pre_linear).astype(BF)
        linear_factor_ref[:, at] = scaled.astype(BF)
        gate_factor_ref[:, at] = (
            pre_linear * logistic * (1.0 + pre_gate * (1.0 - logistic))
        ).astype(BF)


def forward(pieces, gate, linear, deps):
    count = len(pieces)
    size, width = pieces[0].shape
    rows = count * pad16(size)
    hidden = gate[0].shape[1]
    return pl.pallas_call(
        functools.partial(forward_body, count, len(deps)),
        in_specs=[VMEM] * (count + 4) + [ANY] * len(deps),
        out_specs=[VMEM] * 5,
        out_shape=[jax.ShapeDtypeStruct((rows, width), BF)]
        + [jax.ShapeDtypeStruct((rows, hidden), BF)] * 3
        + [jax.ShapeDtypeStruct((8, 128), F32)],
        compiler_params=params(10),
        cost_estimate=cost(4 * rows * width * hidden, 6 * rows * hidden + 4 * width * hidden),
        name="forward_rows",
    )(*pieces, *gate, *linear, *deps)


def backward_body(count, deps, *refs):
    piece_refs = refs[:count]
    gate_factor, linear_factor, out_m, out_o = refs[count : count + 4]
    gate_m, gate_o, linear_m, linear_o = refs[count + 4 : count + 8]
    refs = refs[count + 8 + deps :]
    b_ref, gate_delta_ref, linear_delta_ref = refs[:3]
    row_refs, mark_ref, total = refs[3:-2], refs[-2], refs[-1]
    mark_body(mark_ref)
    assemble(piece_refs, b_ref)
    hidden, half = out_m.shape
    tile = tile_of(hidden)
    for start in range(0, hidden, tile):
        at = slice(start, start + tile)
        grad = lax.dot_general(b_ref[:, :half], out_m[at, :], LAST, preferred_element_type=F32)
        grad += lax.dot_general(b_ref[:, half:], out_o[at, :], LAST, preferred_element_type=F32)
        gate_delta_ref[:, at] = (grad * gate_factor[:, at].astype(F32)).astype(BF)
        linear_delta_ref[:, at] = (grad * linear_factor[:, at].astype(F32)).astype(BF)
    for start, gate, linear in ((0, gate_m, linear_m), (half, gate_o, linear_o)):
        part = lax.dot_general(gate_delta_ref[...], gate[...], LAST, preferred_element_type=F32)
        part += lax.dot_general(
            linear_delta_ref[...], linear[...], LAST, preferred_element_type=F32
        )
        total[:, start : start + half] = part
    size = row_refs[0].shape[0]
    for i, ref in enumerate(row_refs):
        start = i * pad16(size)
        ref[...] = total[start : start + size, :].astype(BF)


def backward(pieces, gate_factor, linear_factor, out, gate, linear, deps):
    count = len(pieces)
    size, width = pieces[0].shape
    rows = count * pad16(size)
    hidden = gate_factor.shape[1]
    results = pl.pallas_call(
        functools.partial(backward_body, count, len(deps)),
        in_specs=[VMEM] * (count + 8) + [ANY] * len(deps),
        out_specs=[VMEM] * (4 + count),
        out_shape=[jax.ShapeDtypeStruct((rows, width), BF)]
        + [jax.ShapeDtypeStruct((rows, hidden), BF)] * 2
        + [jax.ShapeDtypeStruct((size, width), BF)] * count
        + [jax.ShapeDtypeStruct((8, 128), F32)],
        scratch_shapes=[pltpu.VMEM((rows, width), F32)],
        compiler_params=params(10),
        cost_estimate=cost(6 * rows * width * hidden, 8 * rows * hidden + 6 * width * hidden),
        name="backward_rows",
    )(*pieces, gate_factor, linear_factor, *out, *gate, *linear, *deps)
    return results[:3], results[3:-1], results[-1]


def weight_body(groups, kinds, column, add, deps, *refs):
    received = refs[5 * groups]
    out_refs = refs[5 * groups + (1 if add else 0) + deps :]
    mark_body(out_refs[-1])
    width, hidden = refs[0].shape[1], refs[2].shape[1]
    half, tile = width // 2, tile_of(hidden)
    side = slice(column * half, (column + 1) * half)

    @pl.loop(0, hidden // tile)
    def _(j):
        at = pl.ds(pl.multiple_of(j * tile, tile), tile)
        for place, kind in enumerate(kinds):
            total = None
            for g in range(groups):
                x_ref, b_ref, gate_delta, linear_delta, hid = refs[5 * g : 5 * g + 5]
                if kind == "out":
                    a, b = hid[:, at], b_ref[:, side]
                else:
                    a, b = x_ref[:, side], (gate_delta if kind == "gate" else linear_delta)[:, at]
                term = lax.dot_general(a, b, ROWS, preferred_element_type=F32)
                total = term if total is None else total + term
            rows = (at, slice(None)) if kind == "out" else (pl.ds(place * half, half), at)
            if add:
                total = total + received[rows].astype(F32)
                out_refs[place][at if kind == "out" else slice(None), slice(None) if kind == "out" else at] = (
                    total.astype(BF)
                )
            else:
                out_refs[0][rows] = total.astype(BF)


def weight_grads(groups, kinds, column, received, deps):
    hidden = groups[0][2].shape[1]
    half = groups[0][0].shape[1] // 2
    operands = [a for group in groups for a in group] + list(received)
    one = (hidden, half) if kinds == ("out",) else (half, hidden)
    shapes = [one] * len(kinds) if received else [(len(kinds) * one[0], one[1])]
    total_rows = sum(group[0].shape[0] for group in groups)
    return pl.pallas_call(
        functools.partial(
            weight_body, len(groups), kinds, column, bool(received), len(deps)
        ),
        in_specs=[VMEM] * len(operands) + [ANY] * len(deps),
        out_specs=[VMEM] * (len(shapes) + 1),
        out_shape=[jax.ShapeDtypeStruct(s, BF) for s in shapes]
        + [jax.ShapeDtypeStruct((8, 128), F32)],
        compiler_params=params(12),
        cost_estimate=cost(
            2 * len(kinds) * total_rows * half * hidden, 4 * total_rows * hidden
        ),
        name="weight_grads",
    )(*operands, *deps)


def finish_body(count, *refs):
    part_refs, (down_m, down_o), out_ref = refs[:count], refs[count : count + 2], refs[-1]
    total = part_refs[0][...].astype(F32)
    for ref in part_refs[1:]:
        total = total + ref[...].astype(F32)
    total = total.astype(BF)
    model, half = down_m.shape
    tile = tile_of(model)
    for start in range(0, model, tile):
        at = slice(start, start + tile)
        part = lax.dot_general(total[:, :half], down_m[at, :], LAST, preferred_element_type=F32)
        part += lax.dot_general(total[:, half:], down_o[at, :], LAST, preferred_element_type=F32)
        out_ref[:, at] = part.astype(BF)


def finish(parts, down, deps):
    tokens, model = parts[0].shape[0], down[0].shape[0]
    return pl.pallas_call(
        lambda *refs: finish_body(len(parts), *refs[: len(parts) + 2], refs[-1]),
        in_specs=[VMEM] * (len(parts) + 2) + [ANY] * len(deps),
        out_specs=VMEM,
        out_shape=jax.ShapeDtypeStruct((tokens, model), BF),
        compiler_params=params(10),
        cost_estimate=cost(2 * tokens * model * parts[0].shape[1], 4 * down[0].size),
        name="token_grad",
    )(*parts, *down, *deps)


def on_device(
    tokens,
    cotangent,
    expert_ids,
    slot_ids,
    gate_weights,
    latent_down,
    latent_up,
    expert_gate,
    expert_linear,
    expert_out,
):
    row_count = tokens.shape[0]
    pick_count = expert_ids.shape[1]
    group_count = lax.axis_size("expert")
    halves = lax.axis_size("half")
    expert_count = group_count * expert_gate.shape[0]
    capacity = min(
        row_count, 2 * ((9 * row_count * pick_count + 16 * expert_count - 1) // (16 * expert_count))
    )
    inner = group_count // PLANES
    fan = inner // SIDE

    def swap(a):
        return lax.ppermute(a, "dp", [(0, 1), (1, 0)])

    def along(a, shift):
        return lax.ppermute(
            a,
            "expert",
            [
                (z * inner + p, (z + shift) % PLANES * inner + p)
                for z in range(PLANES)
                for p in range(inner)
            ],
        )

    def beside(a):
        return lax.ppermute(a, "expert", [(i, i ^ 1) for i in range(group_count)])

    def across(parts):
        return [parts[0]] + [
            lax.ppermute(parts[k], "expert", [(i, i ^ (SIDE * k)) for i in range(group_count)])
            for k in range(1, fan)
        ]

    def summed(a):
        return lax.psum(a, "half") if halves > 1 else a

    last = []

    def deps(*extra):
        return [*last[-1:], *extra]

    def step(result):
        last.append(result[0] if isinstance(result, (list, tuple)) else result)
        return result

    def dot(a, weight, dims):
        if last:
            a = lax.optimization_barrier((a, last[-1]))[0]
        result = lax.dot_general(a, weight, dims, preferred_element_type=F32)
        return step(summed(result).astype(BF))

    def swapped_after(arrays, extra):
        held = lax.optimization_barrier((*arrays, *extra))[: len(arrays)]
        return [(a, swap(a)) for a in held]

    their_tokens, their_cotangent = swap(tokens), swap(cotangent)
    rows_first = (((1,), (0,)), ((), ()))
    latent_own = dot(tokens, latent_down, rows_first)
    latent_other = swap(dot(their_tokens, latent_down, rows_first))
    latent = step(
        join_rows(
            latent_own, latent_other, (expert_ids.T, slot_ids.T, gate_weights.T), deps()
        )
    )
    gate, linear, out = swapped_after(
        (expert_gate[0], expert_linear[0], expert_out[0]), (latent,)
    )
    back_own = dot(cotangent, latent_up, LAST)
    back_other = swap(dot(their_cotangent, latent_up, LAST))

    blocks, pairs, pieces = {("l", 0): latent}, {}, {}

    def to_plane(kind, c, *extra):
        block = blocks[kind, 0]
        if extra:
            block = step(tie(block, deps(*extra)))
        with jax.named_scope(f"plane_{kind}{c}"):
            blocks[kind, c] = along(block, c)

    def to_side(kind, c, tied=False):
        if tied:
            blocks[kind, c] = step(tie(blocks[kind, c], deps()))
        with jax.named_scope(f"side_{kind}{c}"):
            pairs[kind, c] = [blocks[kind, c], beside(blocks[kind, c])]

    def pick(kind, c, *extra):
        parts = step(
            select(
                pairs["l", c], pairs[kind, c], pick_count, fan, capacity, kind == "b", deps(*extra)
            )
        )
        with jax.named_scope(f"piece_{kind}{c}"):
            pieces[kind, c] = across(parts)

    def come(kind, c):
        return pieces[kind, c][-1]

    factors, saved, rows, partial = {}, {}, {}, {}

    def ahead(chunks):
        *factors[chunks], mark = forward(
            [a for c in chunks for a in pieces["l", c]], gate, linear, deps()
        )
        step(mark)

    def behind(chunks, *extra):
        x, gate_factor, linear_factor, hid = factors[chunks]
        (b, gate_delta, linear_delta), sums, mark = backward(
            [a for c in chunks for a in pieces["b", c]],
            gate_factor,
            linear_factor,
            out,
            gate,
            linear,
            deps(*extra),
        )
        step(mark)
        saved[chunks] = (x, b, gate_delta, linear_delta, hid)
        for i, c in enumerate(chunks):
            rows[c] = sums[i * fan : (i + 1) * fan]

    def send_rows(c, operands):
        with jax.named_scope(f"piece_r{c}"):
            rows[c] = across([rows[c][0], *operands])

    def send_side(c, results):
        own, other = results
        with jax.named_scope(f"side_r{c}"):
            partial[c] = [own, beside(other)]

    def send_home(c, results):
        with jax.named_scope(f"plane_r{c}"):
            partial[c] = along(results[0], -c)

    def turn(parts, through=(), extra=()):
        results, passed = bundle(parts, list(through), deps(*extra))
        step(results[0][0])
        return [*results, *passed]

    def gathered(c):
        return expanded(pairs["l", c], rows[c], pick_count, capacity, [F32, BF])

    to_plane("l", 1)
    to_side("l", 0)
    to_plane("l", 3, gate[1])
    back = step(join_rows(back_own, back_other, (), deps()))
    blocks["b", 0] = back
    pick("l", 0, blocks["l", 1], linear[1], out[1])
    to_side("l", 1)
    to_plane("l", 2, blocks["l", 1])
    pick("l", 1, blocks["l", 3])
    to_side("l", 3)
    to_plane("b", 2, blocks["l", 3])
    pick("l", 3, come("l", 0))
    to_side("b", 0)
    pick("b", 0, come("l", 1))
    to_side("l", 2)
    to_plane("b", 3, blocks["l", 2])
    ahead((0, 1))
    pick("l", 2, come("l", 3), blocks["b", 2])
    to_side("b", 2)
    to_plane("b", 1, blocks["b", 2])
    (down,) = swapped_after((latent_down,), last[-1:])
    pick("b", 2, come("b", 0), blocks["b", 3])
    to_side("b", 3)
    pick("b", 3, come("l", 2), blocks["b", 1])
    to_side("b", 1)
    ahead((3, 2))
    pick("b", 1, come("b", 2))
    behind((3, 2))
    send_rows(3, rows[3][1:])
    behind((0, 1))
    results = turn([gathered(3), copies(rows[2][1:])])
    send_side(3, results[0])
    send_rows(2, results[1])
    groups = list(saved.values())

    def grads_of(kinds, column, *received):
        *results, mark = weight_grads(groups, kinds, column, received, deps())
        step(mark)
        return results

    wide = grads_of(("gate", "linear"), 1)
    results = turn([gathered(2), added(partial[3], BF), copies(rows[1][1:])], wide)
    send_side(2, results[0])
    send_home(3, results[1])
    send_rows(1, results[2])
    wide = swap(results[3])
    tall = grads_of(("out",), 1)
    results = turn([gathered(1), added(partial[2], BF), copies(rows[0][1:])], tall, [partial[3]])
    send_side(1, results[0])
    send_home(2, results[1])
    send_rows(0, results[2])
    tall = swap(results[3])
    grads = grads_of(("gate", "linear"), 0, wide)
    results = turn([gathered(0), added(partial[1], BF)], (), [])
    send_side(0, results[0])
    send_home(1, results[1])
    grads += grads_of(("out",), 0, tall)
    parts = [*partial[0], partial[1], partial[2], partial[3]]
    if halves > 1:
        results = turn([added(parts, F32)])
        parts = [summed(results[0][0])]
    token_grad = finish(parts, down, deps())
    return (token_grad, grads[0][None], grads[1][None], grads[2][None])


def solution(mesh):
    in_specs = (
        P(("expert", "dp"), "half"),
        P(("expert", "dp"), "half"),
        P(("expert", "dp"), None),
        P(("expert", "dp"), None),
        P(("expert", "dp"), None),
        P("half", "dp"),
        P("dp", "half"),
        P("expert", "dp", "half"),
        P("expert", "dp", "half"),
        P("expert", "half", "dp"),
    )
    out_specs = (
        P(("expert", "dp"), "half"),
        P("expert", "dp", "half"),
        P("expert", "dp", "half"),
        P("expert", "half", "dp"),
    )
    return jax.shard_map(
        on_device, mesh=mesh, in_specs=in_specs, out_specs=out_specs, check_vma=False
    )
```
